32 devices in a mesh: seq: 2 (over x), fsdp: 4 (over z), tensor: 4 (over y, core).
Axes of the slice: x: 2, y: 2, z: 4, core: 2. Of those that a mesh axis runs over, the one named last changes fastest.
Arguments:
- layer_in: bfloat16 [1, 5120, 2304], P(None, ('seq', 'fsdp')), may hold values from -6 to 6
- segment_ids: int32 [1, 5120], replicated, may hold values from 0 to 3, as said below
- attn_pre_gain: bfloat16 [2304], P('fsdp'), may hold values from 0.099609375 to 1.8984375
- query_weight: bfloat16 [2304, 2048], P('fsdp', 'tensor'), may hold values from -0.125 to 0.125
- key_weight: bfloat16 [2304, 1024], P('fsdp', 'tensor'), may hold values from -0.125 to 0.125
- value_weight: bfloat16 [2304, 1024], P('fsdp', 'tensor'), may hold values from -0.125 to 0.125
- out_weight: bfloat16 [2048, 2304], P('tensor', 'fsdp'), may hold values from -0.125 to 0.125
- attn_post_gain: bfloat16 [2304], P('fsdp'), may hold values from 0.099609375 to 1.8984375
- ffn_pre_gain: bfloat16 [2304], P('fsdp'), may hold values from 0.099609375 to 1.8984375
- gate_weight: bfloat16 [2304, 9216], P('fsdp', 'tensor'), may hold values from -0.125 to 0.125
- up_weight: bfloat16 [2304, 9216], P('fsdp', 'tensor'), may hold values from -0.125 to 0.125
- down_weight: bfloat16 [9216, 2304], P('tensor', 'fsdp'), may hold values from -0.0625 to 0.0625
- ffn_post_gain: bfloat16 [2304], P('fsdp'), may hold values from 0.099609375 to 1.8984375
- out_grad: bfloat16 [1, 5120, 2304], P(None, ('seq', 'fsdp')), may hold values from -6 to 6
Outputs:
- layer_out: bfloat16 [1, 5120, 2304], P(None, ('seq', 'fsdp'))
- input_grad: float32 [1, 5120, 2304], P(None, ('seq', 'fsdp'))
- attn_pre_gain_grad: float32 [2304], P('fsdp')
- query_weight_grad: float32 [2304, 2048], P('fsdp', 'tensor')
- key_weight_grad: float32 [2304, 1024], P('fsdp', 'tensor')
- value_weight_grad: float32 [2304, 1024], P('fsdp', 'tensor')
- out_weight_grad: float32 [2048, 2304], P('tensor', 'fsdp')
- attn_post_gain_grad: float32 [2304], P('fsdp')
- ffn_pre_gain_grad: float32 [2304], P('fsdp')
- gate_weight_grad: float32 [2304, 9216], P('fsdp', 'tensor')
- up_weight_grad: float32 [2304, 9216], P('fsdp', 'tensor')
- down_weight_grad: float32 [9216, 2304], P('tensor', 'fsdp')
- ffn_post_gain_grad: float32 [2304], P('fsdp')
The draws below stay inside these ranges and needn't reach their ends.
Inputs may be any that keep to these rules, and one draw needn't show every extreme that they name: `segment_ids`: along each sequence the ids start at 0 and rise by one at each document start; every sequence holds four documents, and the starts of the second to fourth lie within the last 640 tokens.
All inputs are finite; a program needn't handle non-finite values.
Results may differ from the reference program's by a relative error of at most 0.022.
Values may be sent and summed in bfloat16 or wider, within the bound.
No kernel may reach another device: no remote copies, remote signals or barrier semaphores. Data moves between devices by JAX's collectives and lax.ppermute only.
A program may use at most 320 MiB of HBM per device.

```python
import math
import jax
import jax.numpy as jnp
from jax import lax

D = 2304
H = 8
KV = 4
HD = 256
FF = 9216
WINDOW = 4096
LENGTH = 5120
SEQS = 1
QBLOCK = 512
PIECE = 640


doc_cuts = 3


def draw_segment_ids(key, part):
    key = jax.random.fold_in(key, 7)

    def cuts_of(sub_key):
        return jax.random.permutation(sub_key, PIECE - 1)[:doc_cuts] + (LENGTH - PIECE + 1)
    cut_points = jax.vmap(cuts_of)(jax.random.split(key, SEQS)).astype(jnp.int32)
    places = jnp.arange(LENGTH, dtype=jnp.int32)
    counted = jnp.sum((places[None, :, None] >= cut_points[:, None, :]).astype(jnp.int32), axis=-1)
    return counted.astype(jnp.int32)


def raised(values, key, source, target, shards_of, factor):
    owner, partner = [(jnp.arange(values.shape[axis_at]) // (values.shape[axis_at] // shards_of)).reshape([-1 if axis == axis_at else 1 for axis in range(values.ndim)]) for axis_at in (source, target)]
    chosen = jax.random.permutation(key, shards_of)[partner]
    strong = (owner == chosen) | (owner == (partner + shards_of // 2) % shards_of)
    return jnp.where(strong, factor * values, values)


def steps_of(rng, dims, cuts, smallest, high):
    def one(dim, blocks):
        draws = jax.random.uniform(jax.random.fold_in(jax.random.fold_in(rng, 6), dim), (blocks,), jnp.float32, smallest / len(cuts), high / len(cuts))
        return jnp.repeat(jnp.exp(draws), dims[dim] // blocks).reshape((-1,) + (1,) * (len(dims) - dim - 1))

    level = one(*cuts[0])
    for cut in cuts[1:]:
        level = level * one(*cut)
    return level


def normal_values(key, shape, deviation, bound, cuts=(), kind=jnp.bfloat16):
    level = steps_of(key, shape, cuts, -0.22, 0.18) if cuts else 1.0
    entries = jax.random.normal(key, shape, jnp.float32) * deviation * level
    return jnp.minimum(jnp.maximum(entries, -bound), bound).astype(kind)


def gaussian_with(key, extent, deviation, bound, cuts, heavy, held_as=jnp.bfloat16):
    values = deviation * jax.random.normal(key, extent, jnp.float32)
    if cuts:
        values = values * steps_of(key, extent, cuts, -0.22, 0.18)
    return jnp.clip(raised(values, jax.random.fold_in(key, 3), *heavy), -bound, bound).astype(held_as)


def setup_inputs(seed: int = 0) -> dict:
    seeds = jax.random.split(jax.random.key(seed), 15)
    layer_in = normal_values(seeds[0], (SEQS, LENGTH, D), 1.0, 6.0, ((1, 8),))
    segment_ids = draw_segment_ids(jax.random.fold_in(seeds[14], 71), 0)
    attn_pre_gain = jnp.clip(1.0 + 0.18 * jax.random.normal(seeds[2], (D,), jnp.float32), 0.099609375, 1.8984375).astype(jnp.bfloat16)
    query_weight = normal_values(seeds[3], (D, H * HD), D ** -0.5, 0.125, ((0, 4), (1, 4)))
    key_weight = normal_values(seeds[4], (D, KV * HD), D ** -0.5, 0.125, ((0, 4), (1, 4)))
    value_weight = normal_values(seeds[5], (D, KV * HD), D ** -0.5, 0.125, ((0, 4), (1, 4)))
    out_weight = normal_values(seeds[6], (H * HD, D), (H * HD) ** -0.5, 0.125, ((0, 4), (1, 4)))
    attn_post_gain = jnp.clip(1.0 + 0.18 * jax.random.normal(seeds[7], (D,), jnp.float32), 0.099609375, 1.8984375).astype(jnp.bfloat16)
    ffn_pre_gain = jnp.clip(1.0 + 0.18 * jax.random.normal(seeds[8], (D,), jnp.float32), 0.099609375, 1.8984375).astype(jnp.bfloat16)
    gate_weight = normal_values(seeds[9], (D, FF), D ** -0.5, 0.125, ((0, 4), (1, 4)))
    up_weight = normal_values(seeds[10], (D, FF), D ** -0.5, 0.125, ((0, 4), (1, 4)))
    down_weight = normal_values(seeds[11], (FF, D), FF ** -0.5, 0.0625, ((0, 4), (1, 4)))
    ffn_post_gain = jnp.clip(1.0 + 0.18 * jax.random.normal(seeds[12], (D,), jnp.float32), 0.099609375, 1.8984375).astype(jnp.bfloat16)
    out_grad = gaussian_with(seeds[13], (SEQS, LENGTH, D), 1.0, 6.0, ((1, 8),), (1, 2, 8, 2.0))
    return {"layer_in": layer_in, "segment_ids": segment_ids, "attn_pre_gain": attn_pre_gain, "query_weight": query_weight, "key_weight": key_weight, "value_weight": value_weight, "out_weight": out_weight, "attn_post_gain": attn_post_gain, "ffn_pre_gain": ffn_pre_gain, "gate_weight": gate_weight, "up_weight": up_weight, "down_weight": down_weight, "ffn_post_gain": ffn_post_gain, "out_grad": out_grad}


epsilon = 1e-06
soft_cap = 50.0
highest = lax.Precision.HIGHEST

@jax.custom_vjp
def low(v):
    return lax.optimization_barrier(v.astype(jnp.bfloat16)).astype(jnp.float32)

@jax.custom_vjp
def low_back(v):
    return v

def low_keep(v):
    return (low(v), None)

def low_pass(kept, grad):
    return (grad,)

def back_keep(v):
    return (v, None)

def back_low(kept, grad):
    return (low(grad),)
low.defvjp(low_keep, low_pass)
low_back.defvjp(back_keep, back_low)

def both_round(field):
    return low(low_back(field))

def rms_norm(field, gain_vec):
    return field * lax.rsqrt(lax.optimization_barrier(jnp.mean(field * field, axis=-1, keepdims=True)) + epsilon) * gain_vec

def tables(positions):
    frequency = jnp.exp(jnp.arange(HD // 2, dtype=jnp.float32) * (-2.0 * math.log(10000.0) / HD))
    angles = positions[:, None] * frequency[None, :]
    return (jnp.cos(angles), jnp.sin(angles))

def rotate(field, cos_tab, sine_tab):
    half_dim = field.shape[-1] // 2
    front_part = field[..., :half_dim]
    back_part = field[..., half_dim:]
    cos_b = cos_tab[:, None, :]
    sin_b = sine_tab[:, None, :]
    return jnp.concatenate([front_part * cos_b - back_part * sin_b, back_part * cos_b + front_part * sin_b], axis=-1)

def attention(queries, keys, values, segment_ids):
    block_count = LENGTH // QBLOCK
    span_len = WINDOW + QBLOCK
    group_size = H // KV

    def attend_block(block_index):
        row_index = block_index // block_count
        q_start = block_index % block_count * QBLOCK
        k_start = jnp.clip(q_start - WINDOW, 0, LENGTH - span_len)
        anchor = jnp.zeros((), jnp.int32)
        q_block = lax.dynamic_slice(queries, (row_index, q_start, anchor, anchor), (1, QBLOCK, H, HD))[0]
        k_block = lax.dynamic_slice(keys, (row_index, k_start, anchor, anchor), (1, span_len, KV, HD))[0]
        v_block = lax.dynamic_slice(values, (row_index, k_start, anchor, anchor), (1, span_len, KV, HD))[0]
        q_seg = lax.dynamic_slice(segment_ids, (row_index, q_start), (1, QBLOCK))[0]
        k_seg = lax.dynamic_slice(segment_ids, (row_index, k_start), (1, span_len))[0]
        offsets = (q_start + jnp.arange(QBLOCK, dtype=jnp.int32))[:, None] - (k_start + jnp.arange(span_len, dtype=jnp.int32))[None, :]
        allowed = (offsets >= 0) & (offsets < WINDOW) & (q_seg[:, None] == k_seg[None, :])
        grouped = q_block.reshape(QBLOCK, KV, group_size, HD)
        raw_scores = low_back(jnp.einsum('qgrd,kgd->grqk', grouped, k_block, precision=highest))
        capped = jnp.where(allowed[None, None], soft_cap * jnp.tanh(raw_scores / soft_cap), -1e+30)
        attn_probs = jax.nn.softmax(capped, axis=-1)
        mixed = jnp.einsum('grqk,kgd->qgrd', low(attn_probs), v_block, precision=highest)
        return mixed.reshape(QBLOCK, H * HD)
    indices = jnp.arange(SEQS * block_count, dtype=jnp.int32)
    outputs = lax.map(jax.checkpoint(attend_block), indices)
    return outputs.reshape(SEQS * LENGTH, H * HD)

def reference(layer_in, segment_ids, attn_pre_gain, query_weight, key_weight, value_weight, out_weight, attn_post_gain, ffn_pre_gain, gate_weight, up_weight, down_weight, ffn_post_gain, out_grad):
    token_count = SEQS * LENGTH
    positions = jnp.arange(LENGTH, dtype=jnp.int32).astype(jnp.float32)
    cos_tab, sine_tab = tables(positions)
    q_scale = HD ** (-0.5)

    def forward_layer(inputs, pre_gain, w_query, w_key, w_value, w_out, post_gain, mlp_pre, w_gate, w_up, w_down, mlp_post):
        flat = inputs.reshape(token_count, D)
        h_one = low(rms_norm(flat, pre_gain))
        q_pre = low_back(jnp.dot(h_one, w_query, precision=highest)).reshape(SEQS, LENGTH, H, HD)
        k_pre = low_back(jnp.dot(h_one, w_key, precision=highest)).reshape(SEQS, LENGTH, KV, HD)
        v_cast = both_round(jnp.dot(h_one, w_value, precision=highest)).reshape(SEQS, LENGTH, KV, HD)
        q_cast = low(rotate(q_pre, cos_tab, sine_tab) * q_scale)
        k_cast = low(rotate(k_pre, cos_tab, sine_tab))
        attended = both_round(attention(q_cast, k_cast, v_cast, segment_ids))
        a_sum = low_back(jnp.dot(attended, w_out, precision=highest))
        r_one = flat + rms_norm(a_sum, post_gain)
        h_two = low(rms_norm(r_one, mlp_pre))
        gate_pre = low_back(jnp.dot(h_two, w_gate, precision=highest))
        up_pre = low_back(jnp.dot(h_two, w_up, precision=highest))
        hidden = low(jax.nn.gelu(gate_pre, approximate=True) * up_pre)
        m_sum = low_back(jnp.dot(hidden, w_down, precision=highest))
        return (r_one + rms_norm(m_sum, mlp_post)).reshape(SEQS, LENGTH, D)
    result, pullback = jax.vjp(forward_layer, layer_in.astype(jnp.float32), attn_pre_gain.astype(jnp.float32), query_weight.astype(jnp.float32), key_weight.astype(jnp.float32), value_weight.astype(jnp.float32), out_weight.astype(jnp.float32), attn_post_gain.astype(jnp.float32), ffn_pre_gain.astype(jnp.float32), gate_weight.astype(jnp.float32), up_weight.astype(jnp.float32), down_weight.astype(jnp.float32), ffn_post_gain.astype(jnp.float32))
    input_grad, pre_grad, query_grad, key_grad, value_grad, out_w_grad, post_grad, mlp_pre_grad, gate_grad, up_grad, down_grad, mlp_post_grad = pullback(out_grad.astype(jnp.float32))
    return (result.astype(jnp.bfloat16), input_grad, pre_grad, query_grad, key_grad, value_grad, out_w_grad, post_grad, mlp_pre_grad, gate_grad, up_grad, down_grad, mlp_post_grad)
```

```python
import functools
import math

import jax
import jax.numpy as jnp
from jax import lax
from jax.experimental import pallas as pl
from jax.experimental.pallas import tpu as pltpu
from jax.sharding import PartitionSpec as P

HD = 256
WINDOW = 4096
epsilon = 1e-06
soft_cap = 50.0
f32 = jnp.float32
bf16 = jnp.bfloat16


def swap(value, axis, bit=1):
    return lax.ppermute(value, axis, [(i, i ^ bit) for i in range(lax.axis_size(axis))])


def swap_x(value):
    return swap(value, "seq")


def swap_y(value):
    return swap(value, "tensor", 2)


def swap_core(value):
    return swap(value, "tensor", 1)


def swap_z(value):
    return swap(value, "fsdp", 1)


def turn(value):
    size = lax.axis_size("fsdp")
    return lax.ppermute(value, "fsdp", [(i, (i + 1) % size) for i in range(size)])


def gather8(own):
    cut = own.shape[1] // 2
    a, b = own[:, :cut], own[:, cut:]
    a = jnp.stack([a, swap_x(a)])
    b = jnp.stack([b, swap_y(b)])
    a = jnp.stack([a, swap_y(a)])
    b = jnp.stack([b, swap_x(b)], axis=1)
    chip = jnp.concatenate([a, b], axis=-1)
    return jnp.stack([chip, swap_core(chip)]).reshape(8 * own.shape[0], -1)


def send(part, mover):
    return mover(part.astype(bf16)).astype(f32)


def scatter8(part):
    rows, width = part.shape[0] // 8, part.shape[1]
    cut = width // 2
    part = part.reshape(2, 2, 2, rows, width)
    part = part[0] + send(part[1], swap_core)
    a, b = part[..., :cut], part[..., cut:]
    a = a[:, 0] + send(a[:, 1], swap_x)
    b = b[0] + send(b[1], swap_y)
    a = a[0] + send(a[1], swap_y)
    b = b[0] + send(b[1], swap_x)
    return jnp.concatenate([a, b], axis=-1)


def gather16(own):
    cut = own.shape[1] // 3
    a, b, c = own[:, :cut], own[:, cut : 2 * cut], own[:, 2 * cut :]
    a, b, c = (jnp.stack([a, swap_x(a)]), jnp.stack([b, swap_y(b)]), jnp.stack([c, swap_z(c)]))
    a, b, c = (
        jnp.stack([a, swap_y(a)]),
        jnp.stack([b, swap_z(b)]),
        jnp.stack([c, swap_x(c)], axis=1),
    )
    a, b, c = (
        jnp.stack([a, swap_z(a)]),
        jnp.stack([b, swap_x(b)], axis=2),
        jnp.stack([c, swap_y(c)], axis=1),
    )
    chip = jnp.concatenate([a, b, c], axis=-1)
    return jnp.stack([chip, swap_core(chip)]).reshape(16 * own.shape[0], -1)


def scatter16(keep, give):
    rows, width = keep.shape[0] // 8, keep.shape[1]
    cut = width // 3
    part = (keep + send(give, swap_core)).reshape(2, 2, 2, rows, width)
    a, b, c = part[..., :cut], part[..., cut : 2 * cut], part[..., 2 * cut :]
    a = a[0] + send(a[1], swap_z)
    b = b[:, :, 0] + send(b[:, :, 1], swap_x)
    c = c[:, 0] + send(c[:, 1], swap_y)
    a = a[0] + send(a[1], swap_y)
    b = b[0] + send(b[1], swap_z)
    c = c[:, 0] + send(c[:, 1], swap_x)
    a = a[0] + send(a[1], swap_x)
    b = b[0] + send(b[1], swap_y)
    c = c[0] + send(c[1], swap_z)
    return jnp.concatenate([a, b, c], axis=-1)


def rms_norm(field, gain_vec):
    return field * lax.rsqrt(jnp.mean(field * field, axis=-1, keepdims=True) + epsilon) * gain_vec


def norm_back(field, gain_vec, incoming):
    unused, pullback = jax.vjp(rms_norm, field, gain_vec)
    return pullback(incoming)


def tables(positions):
    frequency = jnp.exp(jnp.arange(HD // 2, dtype=f32) * (-2.0 * math.log(10000.0) / HD))
    angles = positions[..., None] * frequency
    return (jnp.cos(angles), jnp.sin(angles))


def rotate(field, cos_tab, sine_tab):
    half_dim = field.shape[-1] // 2
    front, back = field[..., :half_dim], field[..., half_dim:]
    return jnp.concatenate(
        [front * cos_tab - back * sine_tab, back * cos_tab + front * sine_tab], axis=-1
    )


def dot(left, right, dims):
    return lax.dot_general(left, right, (dims, ((), ())), preferred_element_type=f32)


def nn(left, right):
    return dot(left, right, ((1,), (0,)))


def nt(left, right):
    return dot(left, right, ((1,), (1,)))


def tn(left, right):
    return dot(left, right, ((0,), (0,)))


def block_place(info, zs, rows, block):
    x, z = info[0], info[1]
    piece, step = pl.program_id(0), pl.program_id(1)
    home = jnp.where(piece == 0, x, 1 - x) * zs + z
    first = home * rows + step * block
    return x, z, home, first, info[2 + step]


def key_loop(info, zs, rows, block, masked, plain):
    x, z, home, first, first_doc = block_place(info, zs, rows, block)
    last = 2 * zs - 1
    low = jnp.maximum(first - (WINDOW - 1), 0) // rows
    low = jnp.where((home == last) & (first_doc > 0), last, low)

    def visit(g, carry):
        half = (g >= zs).astype(jnp.int32)
        ring = lax.rem(z - (g - half * zs) + zs, zs)
        far = first + block - 1 - g * rows >= WINDOW
        need = (g == home) | far | (home == last)

        @pl.when(need)
        def _():
            masked(x, ring, half, home, g, first)

        @pl.when(jnp.logical_not(need))
        def _():
            plain(x, ring, half, home, g, first)

        return carry

    lax.fori_loop(low, home + 1, visit, 0)


def forward_kernel(zs, rows, block, info, q_ref, kv_ref, col_ref, row_ref, o_ref, lse_ref, acc, tot):
    acc[...] = jnp.zeros_like(acc)
    tot[...] = jnp.zeros_like(tot)
    last = 2 * zs - 1

    def visit(with_mask, x, ring, half, home, g, first):
        raw = nt(q_ref[0], kv_ref[x, ring, half])
        weight = jnp.exp(soft_cap * jnp.tanh(raw * (1.0 / soft_cap)))
        if with_mask:
            row_at = first + lax.broadcasted_iota(jnp.int32, (block, rows), 0)
            col_at = g * rows + lax.broadcasted_iota(jnp.int32, (block, rows), 1)
            gap = row_at - col_at
            row_doc = jnp.where(home == last, col_ref[...], 0)
            col_doc = jnp.where(g == last, row_ref[...], 0)
            weight = jnp.where((gap >= 0) & (gap < WINDOW) & (row_doc == col_doc), weight, 0.0)
        part = weight[:, :128]
        for lane in range(128, rows, 128):
            width = min(128, rows - lane)
            if width < 128:
                tail = jnp.concatenate(
                    [weight[:, lane:], jnp.zeros((block, 128 - width), f32)], axis=1
                )
            else:
                tail = weight[:, lane : lane + 128]
            part = part + tail
        tot[...] += part
        acc[...] += nn(weight.astype(bf16), kv_ref[1 - x, ring, 1 - half])

    key_loop(
        info, zs, rows, block, functools.partial(visit, True), functools.partial(visit, False)
    )
    total = jnp.sum(tot[...], axis=-1, keepdims=True)
    o_ref[0] = (acc[...] / total).astype(bf16)
    lse_ref[0] = jnp.log(total)


def backward_kernel(
    zs, rows, block, info, q_ref, do_ref, lse_ref, delta_ref, kv_ref, col_ref, row_ref, dq_ref, dkv_ref, acc, dkv
):
    piece, step = pl.program_id(0), pl.program_id(1)
    last = 2 * zs - 1

    @pl.when((piece == 0) & (step == 0))
    def _():
        dkv[...] = jnp.zeros_like(dkv)

    acc[...] = jnp.zeros_like(acc)

    def visit(with_mask, x, ring, half, home, g, first):
        q, do = q_ref[0], do_ref[0]
        k, v = kv_ref[x, ring, half], kv_ref[1 - x, ring, 1 - half]
        bent = jnp.tanh(nt(k, q) * (1.0 / soft_cap))
        weight = jnp.exp(soft_cap * bent - lse_ref[0])
        if with_mask:
            row_at = first + lax.broadcasted_iota(jnp.int32, (rows, block), 1)
            col_at = g * rows + lax.broadcasted_iota(jnp.int32, (rows, block), 0)
            gap = row_at - col_at
            row_doc = jnp.where(home == last, row_ref[0], 0)
            col_doc = jnp.where(g == last, col_ref[...], 0)
            weight = jnp.where((gap >= 0) & (gap < WINDOW) & (row_doc == col_doc), weight, 0.0)
        draw = (weight * (nt(v, do) - delta_ref[0]) * (1.0 - bent * bent)).astype(bf16)
        dkv[x, ring, half] += nn(draw, q)
        dkv[1 - x, ring, 1 - half] += nn(weight.astype(bf16), do)
        acc[...] += tn(draw, k)

    key_loop(
        info, zs, rows, block, functools.partial(visit, True), functools.partial(visit, False)
    )
    dq_ref[0] = acc[...]

    @pl.when((piece == 1) & (step == pl.num_programs(1) - 1))
    def _():
        dkv_ref[...] = dkv[...].astype(bf16)


def whole_block(shape):
    return pl.BlockSpec(shape, lambda i, j, info: (0,) * len(shape))


def attend(info, q, kv, doc_col, doc_row, block):
    unused, zs, unused2, rows, unused3 = kv.shape
    steps = rows // block
    return pl.pallas_call(
        functools.partial(forward_kernel, zs, rows, block),
        grid_spec=pltpu.PrefetchScalarGridSpec(
            num_scalar_prefetch=1,
            grid=(2, steps),
            in_specs=[
                pl.BlockSpec((1, block, HD), lambda i, j, info: (i, j, 0)),
                whole_block(kv.shape),
                pl.BlockSpec((block, 1), lambda i, j, info: (j, 0)),
                whole_block((1, rows)),
            ],
            out_specs=[
                pl.BlockSpec((1, block, HD), lambda i, j, info: (i, j, 0)),
                pl.BlockSpec((1, block, 1), lambda i, j, info: (i, j, 0)),
            ],
            scratch_shapes=[pltpu.VMEM((block, HD), f32), pltpu.VMEM((block, 128), f32)],
        ),
        out_shape=[
            jax.ShapeDtypeStruct((2, rows, HD), bf16),
            jax.ShapeDtypeStruct((2, rows, 1), f32),
        ],
        compiler_params=pltpu.CompilerParams(vmem_limit_bytes=48 * 1024 * 1024),
        cost_estimate=pl.CostEstimate(
            flops=4 * 10 * rows * rows * HD, bytes_accessed=8_000_000, transcendentals=20 * rows * rows
        ),
    )(info, q, kv, doc_col, doc_row)


def attend_back(info, q, d_out, lse, delta, kv, doc_col, doc_row, block):
    unused, zs, unused2, rows, unused3 = kv.shape
    steps = rows // block
    piece_block = pl.BlockSpec((1, block, HD), lambda i, j, info: (i, j, 0))
    row_block = pl.BlockSpec((1, 1, block), lambda i, j, info: (i * steps + j, 0, 0))
    return pl.pallas_call(
        functools.partial(backward_kernel, zs, rows, block),
        grid_spec=pltpu.PrefetchScalarGridSpec(
            num_scalar_prefetch=1,
            grid=(2, steps),
            in_specs=[
                piece_block,
                piece_block,
                row_block,
                row_block,
                whole_block(kv.shape),
                whole_block((rows, 1)),
                pl.BlockSpec((1, 1, block), lambda i, j, info: (j, 0, 0)),
            ],
            out_specs=[piece_block, whole_block(kv.shape)],
            scratch_shapes=[pltpu.VMEM((block, HD), f32), pltpu.VMEM(kv.shape, f32)],
        ),
        out_shape=[
            jax.ShapeDtypeStruct((2, rows, HD), f32),
            jax.ShapeDtypeStruct(kv.shape, bf16),
        ],
        compiler_params=pltpu.CompilerParams(vmem_limit_bytes=56 * 1024 * 1024),
        cost_estimate=pl.CostEstimate(
            flops=10 * 10 * rows * rows * HD, bytes_accessed=16_000_000, transcendentals=20 * rows * rows
        ),
    )(info, q, d_out, lse, delta, kv, doc_col, doc_row)


def shards(
    layer_in,
    segment_ids,
    attn_pre_gain,
    query_weight,
    key_weight,
    value_weight,
    out_weight,
    attn_post_gain,
    ffn_pre_gain,
    gate_weight,
    up_weight,
    down_weight,
    ffn_post_gain,
    out_grad,
):
    unused, rows, width = layer_in.shape
    zs, ts = lax.axis_size("fsdp"), lax.axis_size("tensor")
    x, z, t = lax.axis_index("seq"), lax.axis_index("fsdp"), lax.axis_index("tensor")
    b, pair = z % 2, z // 2
    depth = attn_pre_gain.shape[0]
    sub = rows // ts
    quarter = gate_weight.shape[1] // 4
    first = x == 0

    def in_order(parts):
        return jnp.stack(
            [lax.dynamic_index_in_dim(parts, j ^ t, 1, keepdims=False) for j in range(ts)], axis=1
        )

    def to_exchange(pieces):
        parts = in_order(pieces.reshape(2, ts, sub, -1)).reshape(2, 2, 2, sub, -1)
        return parts.transpose(2, 1, 0, 3, 4).reshape(2 * rows, -1)

    def to_sequence(blocks):
        parts = blocks.reshape(2, 2, 2, sub, -1).transpose(2, 1, 0, 3, 4)
        return in_order(parts.reshape(2, ts, sub, -1)).reshape(2, rows, -1)

    gains = jnp.stack([attn_pre_gain, attn_post_gain, ffn_pre_gain, ffn_post_gain])
    all_gains = lax.dynamic_update_slice_in_dim(
        jnp.zeros((zs,) + gains.shape, bf16), gains[None], z, 0
    )
    for j in range(1, zs):
        all_gains = lax.dynamic_update_slice_in_dim(
            all_gains, swap(gains, "fsdp", j)[None], z ^ j, 0
        )
    all_gains = all_gains.transpose(1, 0, 2).reshape(4, width).astype(f32)
    pre_gain, post_gain, mlp_pre, mlp_post = (all_gains[i] for i in range(4))

    own_x = layer_in.reshape(1, ts, sub, width)
    own_x = in_order(own_x)[0].reshape(2, 2, sub, width).transpose(1, 0, 2, 3)
    far_x = swap_x(own_x[0])
    far_x = jnp.stack([far_x, swap_core(far_x)])
    x_rows = jnp.stack([own_x, far_x], axis=2).reshape(2 * rows, width)

    w_qkv = jnp.concatenate(
        [
            lax.dynamic_slice_in_dim(query_weight, x * HD, HD, 1),
            jnp.where(first, key_weight, value_weight),
        ],
        axis=1,
    )
    ring = [w_qkv]
    for unused in range(zs - 1):
        ring.append(turn(ring[-1]))
    w_qkv = jnp.zeros((width, 2 * HD), bf16)
    for i, block in enumerate(ring):
        w_qkv = lax.dynamic_update_slice_in_dim(w_qkv, block, (z - i) % zs * depth, 0)
    w_out = lax.all_gather(
        lax.dynamic_slice_in_dim(out_weight, x * HD, HD, 0).T, "fsdp", axis=0, tiled=True
    )

    def fetch(packs):
        same, other = packs
        whole = jnp.zeros((width, same.shape[1]), bf16)
        for j in range(zs):
            block = same if j == 0 else swap(other if j % 2 else same, "fsdp", j)
            whole = lax.dynamic_update_slice_in_dim(whole, block, (z ^ j) * depth, 0)
        return whole

    def columns(weight, at):
        return lax.dynamic_slice_in_dim(weight, at * quarter, quarter, 1)

    places = (2 * x + b, 2 * x + 1 - b)
    w_gu = fetch(
        [jnp.concatenate([columns(gate_weight, at), columns(up_weight, at)], axis=1) for at in places]
    )
    w_down = fetch(
        [lax.dynamic_slice_in_dim(down_weight, at * quarter, quarter, 0).T for at in places]
    )

    h_one = rms_norm(x_rows.astype(f32), pre_gain).astype(bf16)
    projected = to_sequence(nn(h_one, w_qkv))
    starts = jnp.stack([x * zs + z, (1 - x) * zs + z]) * rows
    positions = starts[:, None] + jnp.arange(rows, dtype=jnp.int32)[None, :]
    cos_tab, sine_tab = tables(positions.astype(f32))
    kv_cos = jnp.where(first, cos_tab, 1.0)
    kv_sine = jnp.where(first, sine_tab, 0.0)
    q_scale = HD ** (-0.5)
    q_cast = (rotate(projected[..., :HD], cos_tab, sine_tab) * q_scale).astype(bf16)
    kv_own = rotate(projected[..., HD:], kv_cos, kv_sine).astype(bf16)
    kv_ring = [kv_own]
    for unused in range(zs - 1):
        kv_ring.append(turn(kv_ring[-1]))
    kv_far = [swap_x(block) for block in kv_ring]
    kv_all = jnp.stack(kv_ring + kv_far).reshape(2, zs, 2, rows, HD)

    block = rows // 2 if rows >= 512 else rows
    last_doc = segment_ids.reshape(2 * zs, rows)[-1]
    info = jnp.concatenate([jnp.stack([x, z]), last_doc[::block]]).astype(jnp.int32)
    doc_col, doc_row = last_doc[:, None], last_doc[None, :]
    mixed, lse = attend(info, q_cast, kv_all, doc_col, doc_row, block)

    o_rows = to_exchange(mixed)
    a_sum = scatter8(nt(o_rows, w_out))

    x_own = lax.dynamic_slice_in_dim(layer_in[0], t * sub, sub, 0).astype(f32)
    r_one = x_own + rms_norm(a_sum, post_gain)
    h_two = gather16(rms_norm(r_one, mlp_pre).astype(bf16))
    gu = nn(h_two, w_gu)
    gate_pre, up_pre = gu[:, :quarter], gu[:, quarter:]
    hidden = (jax.nn.gelu(gate_pre, approximate=True) * up_pre).astype(bf16)
    split = 8 * sub
    m_sum = scatter16(nt(hidden[:split], w_down), nt(hidden[split:], w_down))
    layer_own = (r_one + rms_norm(m_sum, mlp_post)).astype(bf16)
    layer_out = lax.all_gather(layer_own, "tensor", axis=0, tiled=True)[None]

    incoming = lax.dynamic_slice_in_dim(out_grad[0], t * sub, sub, 0).astype(f32)
    d_msum, dg_mlp_post = norm_back(m_sum, mlp_post, incoming)
    dm = gather16(d_msum.astype(bf16))
    d_hidden = nn(dm, w_down)
    unused, gelu_pull = jax.vjp(
        lambda gate_in, up_in: jax.nn.gelu(gate_in, approximate=True) * up_in, gate_pre, up_pre
    )
    d_gate, d_up = gelu_pull(d_hidden)
    d_gu = jnp.concatenate([d_gate.astype(bf16), d_up.astype(bf16)], axis=1)
    dh_two = scatter16(nt(d_gu[:split], w_gu), nt(d_gu[split:], w_gu))
    dw_down = tn(dm, hidden)
    dw_gu = tn(h_two, d_gu)

    dr_add, dg_mlp_pre = norm_back(r_one, mlp_pre, dh_two)
    d_resid = incoming + dr_add
    d_asum, dg_post = norm_back(a_sum, post_gain, d_resid)

    da = gather8(d_asum.astype(bf16))
    d_mixed_rows = nn(da, w_out).astype(bf16)
    d_mixed = to_sequence(d_mixed_rows)
    dw_out = tn(da, o_rows)
    delta = jnp.sum(d_mixed.astype(f32) * mixed.astype(f32), axis=-1)
    steps = rows // block
    d_query, dkv_all = attend_back(
        info,
        q_cast,
        d_mixed,
        lse.reshape(2 * steps, 1, block),
        delta.reshape(2 * steps, 1, block),
        kv_all,
        doc_col,
        doc_row.reshape(steps, 1, block),
        block,
    )
    kept, given = dkv_all[0], dkv_all[1]
    summed = [kept[i].astype(f32) + swap_x(given[i]).astype(f32) for i in range(zs)]
    acc = summed[1] if zs > 1 else summed[0]
    for i in list(range(2, zs)) + [0]:
        acc = send(acc, turn) + summed[i]
    dq_cast = rotate(d_query * q_scale, cos_tab, -sine_tab).astype(bf16)
    dkv_cast = rotate(acc, kv_cos, -kv_sine).astype(bf16)
    d_proj = to_exchange(jnp.concatenate([dq_cast, dkv_cast], axis=-1))
    dh_one = scatter8(nt(d_proj, w_qkv))
    dw_qkv = tn(h_one, d_proj)
    dx_add, dg_pre = norm_back(x_own, pre_gain, dh_one)
    grad_own = (d_resid + dx_add).astype(bf16)
    grad_own = jnp.stack([grad_own, swap_y(grad_own)])
    grad_own = jnp.stack([grad_own, swap_core(grad_own)], axis=1).reshape(1, ts, sub, width)
    input_grad = in_order(grad_own).reshape(1, rows, width).astype(f32)

    def give_back(grad):
        both = 2 * depth
        kept = lax.dynamic_slice_in_dim(grad, pair * both, both, 0)
        for s in range(1, zs // 2):
            part = lax.dynamic_slice_in_dim(grad, (pair ^ s) * both, both, 0)
            kept = kept + swap(part.astype(bf16), "fsdp", 2 * s).astype(f32)
        mine = lax.dynamic_slice_in_dim(kept, b * depth, depth, 0)
        theirs = swap_z(lax.dynamic_slice_in_dim(kept, (1 - b) * depth, depth, 0).astype(bf16))
        far = swap_x(jnp.stack([mine.astype(bf16), theirs]))
        return mine, theirs.astype(f32), far[0].astype(f32), far[1].astype(f32)

    def side_by_side(parts):
        mine, theirs, far_mine, far_theirs = parts
        even = b == 0
        near = jnp.where(
            even, jnp.concatenate([mine, theirs], 1), jnp.concatenate([theirs, mine], 1)
        )
        far = jnp.where(
            even,
            jnp.concatenate([far_mine, far_theirs], 1),
            jnp.concatenate([far_theirs, far_mine], 1),
        )
        return jnp.where(
            first, jnp.concatenate([near, far], 1), jnp.concatenate([far, near], 1)
        )

    g_down = side_by_side(give_back(dw_down)).T
    gu_parts = give_back(dw_gu)
    g_gate = side_by_side([part[:, :quarter] for part in gu_parts])
    g_up = side_by_side([part[:, quarter:] for part in gu_parts])

    def heads(near, far):
        return jnp.where(
            first, jnp.concatenate([near, far], 1), jnp.concatenate([far, near], 1)
        )

    near_out = lax.psum_scatter(dw_out.astype(bf16), "fsdp", scatter_dimension=0, tiled=True)
    g_out = heads(near_out.astype(f32), swap_x(near_out).astype(f32)).T

    def part_of(grad, i):
        return lax.dynamic_slice_in_dim(grad, (z - i) % zs * depth, depth, 0)

    acc = part_of(dw_qkv, 1)
    for i in list(range(2, zs)) + [0]:
        acc = send(acc, turn) + part_of(dw_qkv, i)
    far = swap_x(acc.astype(bf16)).astype(f32)
    g_query = heads(acc[:, :HD], far[:, :HD])
    g_key = jnp.where(first, acc[:, HD:], far[:, HD:])
    g_value = jnp.where(first, far[:, HD:], acc[:, HD:])

    gain_grads = lax.psum(
        jnp.stack([dg_pre, dg_post, dg_mlp_pre, dg_mlp_post]), ("seq", "fsdp", "tensor")
    )
    gain_grads = lax.dynamic_slice_in_dim(gain_grads, z * depth, depth, 1)
    return (
        layer_out,
        input_grad,
        gain_grads[0],
        g_query,
        g_key,
        g_value,
        g_out,
        gain_grads[1],
        gain_grads[2],
        g_gate,
        g_up,
        g_down,
        gain_grads[3],
    )


def solution(mesh):
    return jax.shard_map(
        shards,
        mesh=mesh,
        in_specs=(
            P(None, ("seq", "fsdp"), None),
            P(),
            P("fsdp"),
            P("fsdp", "tensor"),
            P("fsdp", "tensor"),
            P("fsdp", "tensor"),
            P("tensor", "fsdp"),
            P("fsdp"),
            P("fsdp"),
            P("fsdp", "tensor"),
            P("fsdp", "tensor"),
            P("tensor", "fsdp"),
            P("fsdp"),
            P(None, ("seq", "fsdp"), None),
        ),
        out_specs=(
            P(None, ("seq", "fsdp"), None),
            P(None, ("seq", "fsdp"), None),
            P("fsdp"),
            P("fsdp", "tensor"),
            P("fsdp", "tensor"),
            P("fsdp", "tensor"),
            P("tensor", "fsdp"),
            P("fsdp"),
            P("fsdp"),
            P("fsdp", "tensor"),
            P("fsdp", "tensor"),
            P("tensor", "fsdp"),
            P("fsdp"),
        ),
        check_vma=False,
    )
```

```python
import functools
import math

import jax
import jax.numpy as jnp
from jax import lax
from jax.experimental import pallas as pl
from jax.experimental.layout import Layout, with_layout_constraint
from jax.experimental.pallas import tpu as pltpu
from jax.sharding import PartitionSpec as P

HD = 256
WINDOW = 4096
epsilon = 1e-06
soft_cap = 50.0
f32 = jnp.float32
bf16 = jnp.bfloat16


def swap(value, axis, bit=1):
    return lax.ppermute(value, axis, [(i, i ^ bit) for i in range(lax.axis_size(axis))])


def swap_x(value):
    return swap(value, "seq")


def swap_y(value):
    return swap(value, "tensor", 2)


def swap_core(value):
    return swap(value, "tensor", 1)


def turn(value):
    size = lax.axis_size("fsdp")
    return lax.ppermute(value, "fsdp", [(i, (i + 1) % size) for i in range(size)])


class Move:
    def __init__(self, value, mover):
        self.value, self.mover, self.result = value, mover, None


def step(values, begin=(), end=()):
    values, given, taken = lax.optimization_barrier(
        (list(values), [move.value for move in begin], [move.result for move in end])
    )
    for move, value in zip(begin, given):
        move.value, move.result = value, move.mover(value)
    for move, result in zip(end, taken):
        move.result = result
    return values


def at(plan, place, values):
    return step(values, *plan[place]) if place in plan else step(values)


def gather8(own, plan):
    cut = own.shape[1] // 2
    a, b = at(plan, 0, [own[:, :cut], own[:, cut:]])
    a, b = jnp.stack([a, swap_x(a)]), jnp.stack([b, swap_y(b)])
    a, b = at(plan, 1, [a, b])
    a, b = jnp.stack([a, swap_y(a)]), jnp.stack([b, swap_x(b)], axis=1)
    chip = jnp.concatenate([a, b], axis=-1)
    (chip,) = at(plan, 2, [chip])
    return jnp.stack([chip, swap_core(chip)]).reshape(8 * own.shape[0], -1)


def send(part, mover):
    return mover(part.astype(bf16)).astype(f32)


def scatter8(keep, give, plan):
    (given,) = at(plan, 0, [give()])
    part = keep(swap_core(given))
    rows, width = part.shape[0] // 4, part.shape[1]
    cut = width // 2
    part = part.reshape(2, 2, rows, width)
    a, b = part[..., :cut], part[..., cut:]
    give_a, give_b = at(plan, 1, [a[:, 1].astype(bf16), b[1].astype(bf16)])
    a = a[:, 0] + swap_x(give_a).astype(f32)
    b = b[0] + swap_y(give_b).astype(f32)
    give_a, give_b = at(plan, 2, [a[1].astype(bf16), b[1].astype(bf16)])
    a = a[0] + swap_y(give_a).astype(f32)
    b = b[0] + swap_x(give_b).astype(f32)
    return jnp.concatenate([a, b], axis=-1)


def rms_norm(field, gain_vec):
    return field * lax.rsqrt(jnp.mean(field * field, axis=-1, keepdims=True) + epsilon) * gain_vec


def norm_back(field, gain_vec, incoming):
    unused, pullback = jax.vjp(rms_norm, field, gain_vec)
    return pullback(incoming)


def tables(positions):
    frequency = jnp.exp(jnp.arange(HD // 2, dtype=f32) * (-2.0 * math.log(10000.0) / HD))
    angles = positions[..., None] * frequency
    return (jnp.cos(angles), jnp.sin(angles))


def rotate(field, cos_tab, sine_tab):
    half_dim = field.shape[-1] // 2
    front, back = field[..., :half_dim], field[..., half_dim:]
    return jnp.concatenate(
        [front * cos_tab - back * sine_tab, back * cos_tab + front * sine_tab], axis=-1
    )


def dot(left, right, dims):
    return lax.dot_general(left, right, (dims, ((), ())), preferred_element_type=f32)


def nn(left, right):
    return dot(left, right, ((1,), (0,)))


def nt(left, right):
    return dot(left, right, ((1,), (1,)))


def tn(left, right):
    return dot(left, right, ((0,), (0,)))


LIGHT = pl.CostEstimate(flops=500_000_000, bytes_accessed=1_000_000, transcendentals=0)


def block_place(info, zs, rows, block):
    x, z = info[0], info[1]
    piece, step = pl.program_id(0), pl.program_id(1)
    home = jnp.where(piece == 0, x, 1 - x) * zs + z
    first = home * rows + step * block
    return x, z, home, first, info[2 + step]


def key_loop(info, zs, rows, block, masked, plain):
    x, z, home, first, first_doc = block_place(info, zs, rows, block)
    last = 2 * zs - 1
    low = jnp.maximum(first - (WINDOW - 1), 0) // rows
    low = jnp.where((home == last) & (first_doc > 0), last, low)

    def visit(g, carry):
        half = (g >= zs).astype(jnp.int32)
        ring = lax.rem(z - (g - half * zs) + zs, zs)
        far = first + block - 1 - g * rows >= WINDOW
        need = (g == home) | far | (home == last)

        @pl.when(need)
        def _():
            masked(x, ring, half, home, g, first)

        @pl.when(jnp.logical_not(need))
        def _():
            plain(x, ring, half, home, g, first)

        return carry

    lax.fori_loop(low, home + 1, visit, 0)


def forward_kernel(zs, rows, block, info, q_ref, kv_ref, col_ref, row_ref, o_ref, lse_ref, acc, tot):
    acc[...] = jnp.zeros_like(acc)
    tot[...] = jnp.zeros_like(tot)
    last = 2 * zs - 1

    def visit(with_mask, x, ring, half, home, g, first):
        raw = nt(q_ref[0], kv_ref[x, ring, half])
        weight = jnp.exp(soft_cap * jnp.tanh(raw * (1.0 / soft_cap)))
        if with_mask:
            row_at = first + lax.broadcasted_iota(jnp.int32, (block, rows), 0)
            col_at = g * rows + lax.broadcasted_iota(jnp.int32, (block, rows), 1)
            gap = row_at - col_at
            row_doc = jnp.where(home == last, col_ref[...], 0)
            col_doc = jnp.where(g == last, row_ref[...], 0)
            weight = jnp.where((gap >= 0) & (gap < WINDOW) & (row_doc == col_doc), weight, 0.0)
        part = weight[:, :128]
        for lane in range(128, rows, 128):
            width = min(128, rows - lane)
            if width < 128:
                tail = jnp.concatenate(
                    [weight[:, lane:], jnp.zeros((block, 128 - width), f32)], axis=1
                )
            else:
                tail = weight[:, lane : lane + 128]
            part = part + tail
        tot[...] += part
        acc[...] += nn(weight.astype(bf16), kv_ref[1 - x, ring, 1 - half])

    key_loop(
        info, zs, rows, block, functools.partial(visit, True), functools.partial(visit, False)
    )
    total = jnp.sum(tot[...], axis=-1, keepdims=True)
    o_ref[0] = (acc[...] / total).astype(bf16)
    lse_ref[0] = jnp.log(total)


def backward_kernel(
    zs, rows, block, info, q_ref, do_ref, lse_ref, delta_ref, kv_ref, col_ref, row_ref, dq_ref, dkv_ref, acc, dkv
):
    piece, step = pl.program_id(0), pl.program_id(1)
    last = 2 * zs - 1

    @pl.when((piece == 0) & (step == 0))
    def _():
        dkv[...] = jnp.zeros_like(dkv)

    acc[...] = jnp.zeros_like(acc)

    def visit(with_mask, x, ring, half, home, g, first):
        q, do = q_ref[0], do_ref[0]
        k, v = kv_ref[x, ring, half], kv_ref[1 - x, ring, 1 - half]
        bent = jnp.tanh(nt(k, q) * (1.0 / soft_cap))
        weight = jnp.exp(soft_cap * bent - lse_ref[0])
        if with_mask:
            row_at = first + lax.broadcasted_iota(jnp.int32, (rows, block), 1)
            col_at = g * rows + lax.broadcasted_iota(jnp.int32, (rows, block), 0)
            gap = row_at - col_at
            row_doc = jnp.where(home == last, row_ref[0], 0)
            col_doc = jnp.where(g == last, col_ref[...], 0)
            weight = jnp.where((gap >= 0) & (gap < WINDOW) & (row_doc == col_doc), weight, 0.0)
        draw = (weight * (nt(v, do) - delta_ref[0]) * (1.0 - bent * bent)).astype(bf16)
        dkv[x, ring, half] += nn(draw, q)
        dkv[1 - x, ring, 1 - half] += nn(weight.astype(bf16), do)
        acc[...] += tn(draw, k)

    key_loop(
        info, zs, rows, block, functools.partial(visit, True), functools.partial(visit, False)
    )
    dq_ref[0] = acc[...]

    @pl.when((piece == 1) & (step == pl.num_programs(1) - 1))
    def _():
        dkv_ref[...] = dkv[...].astype(bf16)


def whole_block(shape):
    return pl.BlockSpec(shape, lambda i, j, info: (0,) * len(shape))


def attend(info, q, kv, doc_col, doc_row, block):
    unused, zs, unused2, rows, unused3 = kv.shape
    steps = rows // block
    return pl.pallas_call(
        functools.partial(forward_kernel, zs, rows, block),
        grid_spec=pltpu.PrefetchScalarGridSpec(
            num_scalar_prefetch=1,
            grid=(2, steps),
            in_specs=[
                pl.BlockSpec((1, block, HD), lambda i, j, info: (i, j, 0)),
                whole_block(kv.shape),
                pl.BlockSpec((block, 1), lambda i, j, info: (j, 0)),
                whole_block((1, rows)),
            ],
            out_specs=[
                pl.BlockSpec((1, block, HD), lambda i, j, info: (i, j, 0)),
                pl.BlockSpec((1, block, 1), lambda i, j, info: (i, j, 0)),
            ],
            scratch_shapes=[pltpu.VMEM((block, HD), f32), pltpu.VMEM((block, 128), f32)],
        ),
        out_shape=[
            jax.ShapeDtypeStruct((2, rows, HD), bf16),
            jax.ShapeDtypeStruct((2, rows, 1), f32),
        ],
        compiler_params=pltpu.CompilerParams(vmem_limit_bytes=48 * 1024 * 1024),
        cost_estimate=LIGHT,
    )(info, q, kv, doc_col, doc_row)


def attend_back(info, q, d_out, lse, delta, kv, doc_col, doc_row, block):
    unused, zs, unused2, rows, unused3 = kv.shape
    steps = rows // block
    piece_block = pl.BlockSpec((1, block, HD), lambda i, j, info: (i, j, 0))
    row_block = pl.BlockSpec((1, 1, block), lambda i, j, info: (i * steps + j, 0, 0))
    return pl.pallas_call(
        functools.partial(backward_kernel, zs, rows, block),
        grid_spec=pltpu.PrefetchScalarGridSpec(
            num_scalar_prefetch=1,
            grid=(2, steps),
            in_specs=[
                piece_block,
                piece_block,
                row_block,
                row_block,
                whole_block(kv.shape),
                whole_block((rows, 1)),
                pl.BlockSpec((1, 1, block), lambda i, j, info: (j, 0, 0)),
            ],
            out_specs=[piece_block, whole_block(kv.shape)],
            scratch_shapes=[pltpu.VMEM((block, HD), f32), pltpu.VMEM(kv.shape, f32)],
        ),
        out_shape=[
            jax.ShapeDtypeStruct((2, rows, HD), f32),
            jax.ShapeDtypeStruct(kv.shape, bf16),
        ],
        compiler_params=pltpu.CompilerParams(vmem_limit_bytes=56 * 1024 * 1024),
        cost_estimate=LIGHT,
    )(info, q, d_out, lse, delta, kv, doc_col, doc_row)


NN, NT, TN = ((1,), (0,)), ((1,), (1,)), ((0,), (0,))
gelu_slope = math.sqrt(2.0 / math.pi)


def held(shape):
    return pl.BlockSpec(shape, lambda i: (0,) * len(shape), pipeline_mode=pl.Buffered(1))


def row_tiles(tile, columns):
    return pl.BlockSpec((tile, columns), lambda i: (i, 0))


def tiled(body, rows, tile, in_specs, out_columns, out_types, operands):
    return pl.pallas_call(
        body,
        grid=(rows // tile,),
        in_specs=in_specs,
        out_specs=[row_tiles(tile, columns) for columns in out_columns],
        out_shape=[
            jax.ShapeDtypeStruct((rows, columns), kind)
            for columns, kind in zip(out_columns, out_types)
        ],
        compiler_params=pltpu.CompilerParams(vmem_limit_bytes=52 * 1024 * 1024),
        cost_estimate=LIGHT,
    )(*operands)


def product_kernel(dims, count, *refs):
    value = dot(refs[0][...], refs[count][...], dims)
    for i in range(1, count):
        value = value + dot(refs[i][...], refs[count + i][...], dims)
    for added in refs[2 * count : -1]:
        value = value + added[...].astype(f32)
    refs[-1][...] = value.astype(refs[-1].dtype)


def rows_product(lefts, rights, dims, kind, *added):
    lefts, rights = [v if isinstance(v, (list, tuple)) else [v] for v in (lefts, rights)]
    rows = lefts[0].shape[0]
    tile = min(rows, 320)
    columns = rights[0].shape[1 - dims[1][0]]
    specs = [row_tiles(tile, left.shape[1]) for left in lefts]
    specs += [held(right.shape) for right in rights]
    specs += [row_tiles(tile, columns)] * len(added)
    body = functools.partial(product_kernel, dims, len(lefts))
    return tiled(body, rows, tile, specs, [columns], [kind], [*lefts, *rights, *added])[0]


def halves(rows_in):
    return jnp.split(rows_in, 2)


def norm_product_kernel(x_ref, gain_ref, w_ref, h_ref, out_ref):
    field = x_ref[...].astype(f32)
    scale = lax.rsqrt(jnp.mean(field * field, axis=-1, keepdims=True) + epsilon)
    h = (field * scale * gain_ref[...]).astype(bf16)
    h_ref[...] = h
    out_ref[...] = dot(h, w_ref[...], NN)


def norm_product(rows_in, gain, right):
    rows, columns = rows_in.shape
    tile = min(rows, 320)
    specs = [row_tiles(tile, columns), held((1, columns)), held(right.shape)]
    operands = (rows_in, gain[None], right)
    outs, kinds = [columns, right.shape[1]], [bf16, f32]
    return tiled(norm_product_kernel, rows, tile, specs, outs, kinds, operands)


def bend(gate):
    return jnp.tanh(gelu_slope * (gate + 0.044715 * (gate * gate * gate)))


def gated_kernel(h_ref, gate_w, up_w, gate_ref, up_ref, hidden_ref):
    gate = dot(h_ref[...], gate_w[...], NN)
    up = dot(h_ref[...], up_w[...], NN)
    gate_ref[...] = gate
    up_ref[...] = up
    hidden_ref[...] = (0.5 * gate * (1.0 + bend(gate)) * up).astype(bf16)


def gated_product(left, gate_w, up_w):
    rows, depth = left.shape
    tile, columns = min(rows, 160), gate_w.shape[1]
    specs = [row_tiles(tile, depth), held(gate_w.shape), held(up_w.shape)]
    outs, kinds = [columns] * 3, [f32, f32, bf16]
    return tiled(gated_kernel, rows, tile, specs, outs, kinds, (left, gate_w, up_w))


def gated_back_kernel(dm_ref, w_ref, gate_ref, up_ref, d_gate_ref, d_up_ref):
    d_hidden = dot(dm_ref[...], w_ref[...], NN)
    gate, up = gate_ref[...], up_ref[...]
    bent = bend(gate)
    share = 0.5 * (1.0 + bent)
    slope = share + 0.5 * gate * (1.0 - bent * bent) * gelu_slope * (
        1.0 + 3.0 * 0.044715 * (gate * gate)
    )
    d_gate_ref[...] = (d_hidden * up * slope).astype(bf16)
    d_up_ref[...] = (d_hidden * gate * share).astype(bf16)


def gated_back(left, right, gate, up):
    rows, depth = left.shape
    tile, columns = min(rows, 160), gate.shape[1]
    specs = [row_tiles(tile, depth), held(right.shape)] + [row_tiles(tile, columns)] * 2
    outs, kinds = [columns] * 2, [bf16] * 2
    return tiled(gated_back_kernel, rows, tile, specs, outs, kinds, (left, right, gate, up))


def sum_kernel(*refs):
    count = len(refs) // 2
    value = sum(dot(refs[i][...], refs[count + i][...], TN) for i in range(count))
    refs[-1][...] = value.astype(refs[-1].dtype)


def sum_over_rows(pairs, kind=f32):
    lefts, rights = zip(*pairs)
    depth, rows = lefts[0].shape
    tile, columns = 384, rights[0].shape[1]
    left_specs = [pl.BlockSpec((left.shape[0], tile), lambda i: (0, i)) for left in lefts]
    specs = left_specs + [held(right.shape) for right in rights]
    return tiled(sum_kernel, rows, tile, specs, [columns], [kind], lefts + rights)[0]


def shards(
    layer_in,
    segment_ids,
    attn_pre_gain,
    query_weight,
    key_weight,
    value_weight,
    out_weight,
    attn_post_gain,
    ffn_pre_gain,
    gate_weight,
    up_weight,
    down_weight,
    ffn_post_gain,
    out_grad,
):
    unused, rows, width = layer_in.shape
    zs, ts = lax.axis_size("fsdp"), lax.axis_size("tensor")
    x, z, t = lax.axis_index("seq"), lax.axis_index("fsdp"), lax.axis_index("tensor")
    depth = attn_pre_gain.shape[0]
    sub = rows // ts
    units = gate_weight.shape[1] // 2
    first = x == 0

    def in_order(parts):
        return jnp.stack(
            [lax.dynamic_index_in_dim(parts, j ^ t, 1, keepdims=False) for j in range(ts)], axis=1
        )

    def to_exchange(pieces):
        parts = in_order(pieces.reshape(2, ts, sub, -1)).reshape(2, 2, 2, sub, -1)
        return parts.transpose(2, 1, 0, 3, 4).reshape(2 * rows, -1)

    def to_sequence(blocks):
        parts = blocks.reshape(2, 2, 2, sub, -1).transpose(2, 1, 0, 3, 4)
        return in_order(parts.reshape(2, ts, sub, -1)).reshape(2, rows, -1)

    def z_move(value, bits):
        return Move(value, functools.partial(swap, axis="fsdp", bit=bits))

    w_own = jnp.concatenate(
        [
            lax.dynamic_slice_in_dim(query_weight, x * HD, HD, 1),
            jnp.where(first, key_weight, value_weight),
        ],
        axis=1,
    )
    gains = jnp.concatenate([attn_pre_gain, attn_post_gain, ffn_pre_gain, ffn_post_gain])
    gain_rows = -(-4 * depth // (32 * HD)) * 16
    gains = jnp.pad(gains, (0, gain_rows * 2 * HD - 4 * depth)).reshape(gain_rows, 2 * HD)
    w_own = jnp.concatenate([w_own, gains])
    own_x = in_order(layer_in.reshape(1, ts, sub, width))[0]
    own_x = own_x.reshape(2, 2, sub, width).transpose(1, 0, 2, 3)
    w_own, to_far = lax.optimization_barrier((w_own, own_x[0]))
    ring = [w_own]
    far_move = Move(to_far, swap_x)
    far_move.result = swap_x(to_far)
    for i in range(1, zs):
        (block,) = step([ring[-1]], end=[far_move] if i == zs - 1 else [])
        ring.append(turn(block))
    far_x = far_move.result
    far_x = jnp.concatenate([far_x, swap_core(far_x)]).reshape(rows, width)

    def gathered(part):
        return lax.all_gather(part, "fsdp", axis=0, tiled=True)

    gate_w, up_w = (
        Move(lax.dynamic_slice_in_dim(weight, x * units, units, 1), gathered)
        for weight in (gate_weight, up_weight)
    )
    down_w = Move(lax.dynamic_slice_in_dim(down_weight, x * units, units, 0).T, gathered)
    down_w.result = gathered(down_w.value)
    w_out_own = lax.dynamic_slice_in_dim(out_weight, x * HD, HD, 0).T
    out_moves = {j: z_move(w_out_own, j) for j in range(1, zs)}
    def assemble(own, moves):
        whole = jnp.zeros((width, own.shape[1]), bf16)
        whole = lax.dynamic_update_slice_in_dim(whole, own, z * depth, 0)
        for j, parts in moves.items():
            offset = 0
            for part in parts if isinstance(parts, list) else [parts]:
                part = part.result if isinstance(part, Move) else part
                whole = lax.dynamic_update_slice_in_dim(whole, part, (z ^ j) * depth + offset, 0)
                offset += part.shape[0]
        return whole

    w_qkv = jnp.zeros((width, 2 * HD), bf16)
    all_gains = jnp.zeros((zs, 4, depth), bf16)
    for i, part in enumerate(ring):
        place = (z - i) % zs
        w_qkv = lax.dynamic_update_slice_in_dim(w_qkv, part[:depth], place * depth, 0)
        part = part[depth:].reshape(-1)[: 4 * depth].reshape(1, 4, depth)
        all_gains = lax.dynamic_update_slice_in_dim(all_gains, part, place, 0)
    (w_qkv,) = step([w_qkv], begin=[gate_w])
    all_gains = all_gains.transpose(1, 0, 2).reshape(4, width).astype(f32)
    pre_gain, post_gain, mlp_pre, mlp_post = (all_gains[i] for i in range(4))
    h_own, own_part = norm_product(own_x.reshape(rows, width), pre_gain, w_qkv)
    h_far, far_part = norm_product(far_x, pre_gain, w_qkv)
    projected = jnp.stack(
        [part.reshape(2, 2, sub, 2 * HD) for part in (own_part, far_part)], axis=2
    )
    projected = to_sequence(projected)
    starts = jnp.stack([x * zs + z, (1 - x) * zs + z]) * rows
    positions = starts[:, None] + jnp.arange(rows, dtype=jnp.int32)[None, :]
    cos_tab, sine_tab = tables(positions.astype(f32))
    kv_cos = jnp.where(first, cos_tab, 1.0)
    kv_sine = jnp.where(first, sine_tab, 0.0)
    q_scale = HD ** (-0.5)
    q_cast = (rotate(projected[..., :HD], cos_tab, sine_tab) * q_scale).astype(bf16)
    kv_ring, kv_far = [rotate(projected[..., HD:], kv_cos, kv_sine).astype(bf16)], []
    for i in range(zs):
        moves = []
        if i == zs - 1:
            moves = [out_moves[j] for j in range(1, zs - 1)] + [up_w]
        (here,) = step([kv_ring[-1]], begin=moves)
        if i < zs - 1:
            kv_ring.append(turn(here))
        kv_far.append(swap_x(here))
    kv_all = jnp.stack(kv_ring + kv_far).reshape(2, zs, 2, rows, HD)

    block = rows // 2 if rows >= 512 else rows
    last_doc = segment_ids.reshape(2 * zs, rows)[-1]
    info = jnp.concatenate([jnp.stack([x, z]), last_doc[::block]]).astype(jnp.int32)
    doc_col, doc_row = last_doc[:, None], last_doc[None, :]
    early_out, late_out = [out_moves[j] for j in range(1, zs - 1)], [out_moves[zs - 1]]
    q_cast, kv_all = step([q_cast, kv_all], begin=late_out, end=early_out + [gate_w])
    mixed, lse = attend(info, q_cast, kv_all, doc_col, doc_row, block)
    (mixed,) = step([mixed], end=late_out)
    w_out = assemble(w_out_own, out_moves)

    o_rows = to_exchange(mixed)
    o_halves = halves(o_rows)
    a_sum = scatter8(
        lambda got: rows_product(o_halves[0], w_out, NT, f32, got),
        lambda: rows_product(o_halves[1], w_out, NT, bf16),
        {},
    )

    x_own = lax.dynamic_slice_in_dim(layer_in[0], t * sub, sub, 0).astype(f32)
    r_one = x_own + rms_norm(a_sum, post_gain)
    h_two = gather8(rms_norm(r_one, mlp_pre).astype(bf16), {0: ((), [up_w])})
    gate, up, hidden = gated_product(h_two, gate_w.result, up_w.result)
    hidden_halves = halves(hidden)
    m_sum = scatter8(
        lambda got: rows_product(hidden_halves[0], down_w.result, NT, f32, got),
        lambda: rows_product(hidden_halves[1], down_w.result, NT, bf16),
        {},
    )
    layer_own = (r_one + rms_norm(m_sum, mlp_post)).astype(bf16)

    incoming = lax.dynamic_slice_in_dim(out_grad[0], t * sub, sub, 0).astype(f32)
    d_msum, dg_mlp_post = norm_back(m_sum, mlp_post, incoming)
    def scattered(grad):
        return lax.psum_scatter(grad, "fsdp", scatter_dimension=0, tiled=True)

    class Unit:
        def __init__(self, grad):
            self.sum = Move(grad, scattered)
            self.sum.result = scattered(grad)

        def paired(self):
            self.over = [Move(self.sum.result, swap_x)]
            return self.over

        def parts(self):
            (move,) = self.over
            return move.value, move.result

    class Late:
        def __init__(self, places):
            self.places = places

        def __contains__(self, place):
            return place in self.places

        def __getitem__(self, place):
            return self.places[place]()

    def product(pair):
        return sum_over_rows([pair], bf16)

    dm = gather8(d_msum.astype(bf16), {})
    down_work = Move((dm, hidden), product)
    (dm,) = step([dm], begin=[down_work])
    (dm,) = step([dm], end=[down_work])
    down_unit = Unit(down_work.result)
    d_gate, d_up = gated_back(dm, down_w.result, gate, up)
    gate_work, up_work = Move((h_two, d_gate), product), Move((h_two, d_up), product)
    d_halves = list(zip(halves(d_gate), halves(d_up)))
    weights = (gate_w.result, up_w.result)
    dh_two = scatter8(
        lambda got: rows_product(d_halves[0], weights, NT, f32, got),
        lambda: rows_product(d_halves[1], weights, NT, bf16),
        {1: ([gate_work], ()), 2: ([up_work], [gate_work])},
    )
    gate_unit = Unit(gate_work.result)
    dr_add, dg_mlp_pre = norm_back(r_one, mlp_pre, dh_two)
    d_resid = incoming + dr_add
    d_asum, dg_post = norm_back(a_sum, post_gain, d_resid)

    (da,) = step([d_asum.astype(bf16)], end=[up_work, down_unit.sum])
    up_unit = Unit(up_work.result)
    da = gather8(da, {})
    d_mixed = to_sequence(rows_product(da, w_out, NN, bf16))
    out_work = Move((da, o_rows), lambda pair: sum_over_rows([pair]))
    delta = jnp.sum(d_mixed.astype(f32) * mixed.astype(f32), axis=-1)
    steps = rows // block
    layer_y = Move(layer_own, swap_y)
    d_mixed, delta = step([d_mixed, delta], begin=down_unit.paired() + [layer_y, out_work])
    d_query, dkv_all = attend_back(
        info,
        q_cast,
        d_mixed,
        lse.reshape(2 * steps, 1, block),
        delta.reshape(2 * steps, 1, block),
        kv_all,
        doc_col,
        doc_row.reshape(steps, 1, block),
        block,
    )
    (dkv_all,) = step([dkv_all], end=down_unit.over + [out_work])
    q_rows = to_exchange(rotate(d_query * q_scale, cos_tab, -sine_tab).astype(bf16))

    def qkv_grad(rows_in):
        parts = rows_in.reshape(2, 2, 2, sub, HD)
        near = parts[:, :, 0].reshape(rows, HD)
        far = parts[:, :, 1].reshape(rows, HD)
        return sum_over_rows([(h_own, near), (h_far, far)]).reshape(zs, depth, HD)

    def sends(grad):
        moves = [
            z_move(lax.dynamic_index_in_dim(grad, z ^ j, 0, False).astype(bf16), j)
            for j in range(1, zs)
        ]
        return lax.dynamic_index_in_dim(grad, z, 0, False), moves

    def received(pair_of):
        near, moves = pair_of
        for move in moves:
            near = near + move.result.astype(f32)
        return near.astype(bf16)

    kept, given = dkv_all[0], dkv_all[1]
    order = list(range(1, zs)) + [0]
    acc = kept[order[0]].astype(f32) + send(given[order[0]], swap_x)
    for n, i in enumerate(order[1:]):
        moved, far = acc.astype(bf16), given[i]
        if n == 0:
            dw_query = sends(qkv_grad(q_rows))
            query_work = [
                Move(part, lambda part: rows_product(part, w_qkv[:, :HD], NT, f32))
                for part in halves(q_rows)
            ]
            moved, far = step([moved, far], begin=query_work, end=[layer_y, gate_unit.sum])
        if n == 1:
            moved, far = step([moved, far], begin=dw_query[1], end=query_work)
        acc = kept[i].astype(f32) + swap_x(far).astype(f32) + turn(moved).astype(f32)
    dkv_cast = rotate(acc, kv_cos, -kv_sine).astype(bf16)
    kv_rows = to_exchange(dkv_cast)
    (kv_rows,) = step([kv_rows], begin=gate_unit.paired(), end=dw_query[1])
    kv_halves = halves(kv_rows)
    kv_work = Move(kv_rows, qkv_grad)
    out_back = sends(out_work.result.reshape(zs, depth, HD))
    layer_pair = jnp.stack([layer_own, layer_y.result])
    layer_core = Move(layer_pair, swap_core)
    kv_back = []

    def begin_kv():
        kv_back.extend(sends(kv_work.result))
        return kv_back[1] + up_unit.paired(), [kv_work, up_unit.sum] + gate_unit.over

    w_kv = w_qkv[:, HD:]
    dh_one = scatter8(
        lambda got: rows_product(kv_halves[0], w_kv, NT, f32, query_work[0].result, got),
        lambda: rows_product(kv_halves[1], w_kv, NT, bf16, query_work[1].result),
        Late(
            {
                1: lambda: ([kv_work], ()),
                2: begin_kv,
            }
        ),
    )
    dx_add, dg_pre = norm_back(x_own, pre_gain, dh_one)
    grad_own = (d_resid + dx_add).astype(bf16)
    (grad_own,) = step([grad_own], begin=[layer_core] + out_back[1])
    grad_pair = jnp.stack([grad_own, swap_y(grad_own)])
    (grad_pair,) = step([grad_pair], end=kv_back[1])
    qkv_x = Move(jnp.concatenate([received(dw_query), received(kv_back)], 1), swap_x)
    (grad_pair,) = step([grad_pair], begin=[qkv_x])
    out_x = Move(received(out_back), swap_x)
    out_x.result = swap_x(out_x.value)
    grad_all = jnp.stack([grad_pair, swap_core(grad_pair)], axis=1).reshape(1, ts, sub, width)
    input_grad = in_order(grad_all).reshape(1, rows, width).astype(f32)
    layer_all = jnp.stack([layer_pair, layer_core.result], axis=1).reshape(1, ts, sub, width)
    layer_out = in_order(layer_all).reshape(1, rows, width)

    gain_grads = jnp.stack([dg_pre, dg_post, dg_mlp_pre, dg_mlp_post])
    for mover in (swap_y, swap_core, swap_x):
        gain_grads = gain_grads + mover(gain_grads)
    bits = 1
    while bits < zs:
        gain_grads = gain_grads + swap(gain_grads, "fsdp", bits)
        bits *= 2
    gain_grads = lax.dynamic_slice_in_dim(gain_grads, z * depth, depth, 1)

    def two(even, left, right):
        return jnp.where(
            even, jnp.concatenate([left, right], 1), jnp.concatenate([right, left], 1)
        )

    g_down = two(first, *down_unit.parts()).T.astype(f32)
    g_gate = two(first, *gate_unit.parts()).astype(f32)
    g_up = two(first, *up_unit.parts()).astype(f32)
    near, far = qkv_x.value, qkv_x.result
    g_query = two(first, near[:, :HD], far[:, :HD]).astype(f32)
    g_key = jnp.where(first, near[:, HD:], far[:, HD:]).astype(f32)
    g_value = jnp.where(first, far[:, HD:], near[:, HD:]).astype(f32)
    g_out = two(first, out_x.value, out_x.result).T.astype(f32)
    return (
        layer_out,
        input_grad,
        gain_grads[0],
        g_query,
        g_key,
        g_value,
        g_out,
        gain_grads[1],
        gain_grads[2],
        g_gate,
        g_up,
        g_down,
        gain_grads[3],
    )


def solution(mesh):
    return jax.shard_map(
        shards,
        mesh=mesh,
        in_specs=(
            P(None, ("seq", "fsdp"), None),
            P(),
            P("fsdp"),
            P("fsdp", "tensor"),
            P("fsdp", "tensor"),
            P("fsdp", "tensor"),
            P("tensor", "fsdp"),
            P("fsdp"),
            P("fsdp"),
            P("fsdp", "tensor"),
            P("fsdp", "tensor"),
            P("tensor", "fsdp"),
            P("fsdp"),
            P(None, ("seq", "fsdp"), None),
        ),
        out_specs=(
            P(None, ("seq", "fsdp"), None),
            P(None, ("seq", "fsdp"), None),
            P("fsdp"),
            P("fsdp", "tensor"),
            P("fsdp", "tensor"),
            P("fsdp", "tensor"),
            P("tensor", "fsdp"),
            P("fsdp"),
            P("fsdp"),
            P("fsdp", "tensor"),
            P("fsdp", "tensor"),
            P("tensor", "fsdp"),
            P("fsdp"),
        ),
        check_vma=False,
    )
```

```python
import functools
import math

import jax
import jax.numpy as jnp
from jax import lax
from jax.experimental import pallas as pl
from jax.experimental.layout import Layout, with_layout_constraint
from jax.experimental.pallas import tpu as pltpu
from jax.sharding import PartitionSpec as P

HD = 256
WINDOW = 4096
epsilon = 1e-06
soft_cap = 50.0
f32 = jnp.float32
bf16 = jnp.bfloat16


def swap(value, axis, bit=1):
    return lax.ppermute(value, axis, [(i, i ^ bit) for i in range(lax.axis_size(axis))])


def swap_x(value):
    return swap(value, "seq")


def swap_y(value):
    return swap(value, "tensor", 2)


def swap_core(value):
    return swap(value, "tensor", 1)


def turn(value):
    size = lax.axis_size("fsdp")
    return lax.ppermute(value, "fsdp", [(i, (i + 1) % size) for i in range(size)])


class Move:
    def __init__(self, value, mover):
        self.value, self.mover, self.result = value, mover, None


def step(values, begin=(), end=()):
    values, given, taken = lax.optimization_barrier(
        (list(values), [move.value for move in begin], [move.result for move in end])
    )
    for move, value in zip(begin, given):
        move.value, move.result = value, move.mover(value)
    for move, result in zip(end, taken):
        move.result = result
    return values


def at(plan, place, values):
    return step(values, *plan[place]) if place in plan else step(values)


def gather8(own, plan):
    cut = own.shape[1] // 2
    a, b = at(plan, 0, [own[:, :cut], own[:, cut:]])
    a, b = jnp.stack([a, swap_x(a)]), jnp.stack([b, swap_y(b)])
    a, b = at(plan, 1, [a, b])
    a, b = jnp.stack([a, swap_y(a)]), jnp.stack([b, swap_x(b)], axis=1)
    chip = jnp.concatenate([a, b], axis=-1).reshape(4 * own.shape[0], -1)
    (chip,) = at(plan, 2, [chip])
    return chip, swap_core(chip)


def send(part, mover):
    return mover(part.astype(bf16)).astype(f32)


def scatter8(keep, give, plan):
    (given,) = at(plan, 0, [give()])
    part = keep(swap_core(given))
    rows, width = part.shape[0] // 4, part.shape[1]
    cut = width // 2
    part = part.reshape(2, 2, rows, width)
    a, b = part[..., :cut], part[..., cut:]
    give_a, give_b = at(plan, 1, [a[:, 1], b[1]])
    a = a[:, 0].astype(f32) + swap_x(give_a).astype(f32)
    b = b[0].astype(f32) + swap_y(give_b).astype(f32)
    give_a, give_b = at(plan, 2, [a[1].astype(bf16), b[1].astype(bf16)])
    a = a[0] + swap_y(give_a).astype(f32)
    b = b[0] + swap_x(give_b).astype(f32)
    return jnp.concatenate([a, b], axis=-1)


def rms_norm(field, gain_vec):
    return field * lax.rsqrt(jnp.mean(field * field, axis=-1, keepdims=True) + epsilon) * gain_vec


def norm_back(field, gain_vec, incoming):
    unused, pullback = jax.vjp(rms_norm, field, gain_vec)
    return pullback(incoming)


def tables(positions):
    frequency = jnp.exp(jnp.arange(HD // 2, dtype=f32) * (-2.0 * math.log(10000.0) / HD))
    angles = positions[..., None] * frequency
    return (jnp.cos(angles), jnp.sin(angles))


def rotate(field, cos_tab, sine_tab):
    half_dim = field.shape[-1] // 2
    front, back = field[..., :half_dim], field[..., half_dim:]
    return jnp.concatenate(
        [front * cos_tab - back * sine_tab, back * cos_tab + front * sine_tab], axis=-1
    )


def dot(left, right, dims):
    return lax.dot_general(left, right, (dims, ((), ())), preferred_element_type=f32)


def nn(left, right):
    return dot(left, right, ((1,), (0,)))


def nt(left, right):
    return dot(left, right, ((1,), (1,)))


def tn(left, right):
    return dot(left, right, ((0,), (0,)))


LIGHT = pl.CostEstimate(flops=500_000_000, bytes_accessed=1_000_000, transcendentals=0)


def block_place(info, zs, rows, block):
    x, z = info[0], info[1]
    piece, step = pl.program_id(0), pl.program_id(1)
    home = jnp.where(piece == 0, x, 1 - x) * zs + z
    first = home * rows + step * block
    return x, z, home, first, info[2 + step]


def key_loop(info, zs, rows, block, masked, plain):
    x, z, home, first, first_doc = block_place(info, zs, rows, block)
    last = 2 * zs - 1
    low = jnp.maximum(first - (WINDOW - 1), 0) // rows
    low = jnp.where((home == last) & (first_doc > 0), last, low)

    def visit(g, carry):
        half = (g >= zs).astype(jnp.int32)
        ring = lax.rem(z - (g - half * zs) + zs, zs)
        far = first + block - 1 - g * rows >= WINDOW
        need = (g == home) | far | (home == last)

        @pl.when(need)
        def _():
            masked(x, ring, half, home, g, first)

        @pl.when(jnp.logical_not(need))
        def _():
            plain(x, ring, half, home, g, first)

        return carry

    lax.fori_loop(low, home + 1, visit, 0)


def forward_kernel(zs, rows, block, info, q_ref, kv_ref, col_ref, row_ref, o_ref, lse_ref, acc, tot):
    acc[...] = jnp.zeros_like(acc)
    tot[...] = jnp.zeros_like(tot)
    last = 2 * zs - 1

    def visit(with_mask, x, ring, half, home, g, first):
        raw = nt(q_ref[0], kv_ref[x, ring, half])
        weight = jnp.exp(soft_cap * jnp.tanh(raw * (1.0 / soft_cap)))
        if with_mask:
            row_at = first + lax.broadcasted_iota(jnp.int32, (block, rows), 0)
            col_at = g * rows + lax.broadcasted_iota(jnp.int32, (block, rows), 1)
            gap = row_at - col_at
            row_doc = jnp.where(home == last, col_ref[...], 0)
            col_doc = jnp.where(g == last, row_ref[...], 0)
            weight = jnp.where((gap >= 0) & (gap < WINDOW) & (row_doc == col_doc), weight, 0.0)
        part = weight[:, :128]
        for lane in range(128, rows, 128):
            width = min(128, rows - lane)
            if width < 128:
                tail = jnp.concatenate(
                    [weight[:, lane:], jnp.zeros((block, 128 - width), f32)], axis=1
                )
            else:
                tail = weight[:, lane : lane + 128]
            part = part + tail
        tot[...] += part
        acc[...] += nn(weight.astype(bf16), kv_ref[1 - x, ring, 1 - half])

    key_loop(
        info, zs, rows, block, functools.partial(visit, True), functools.partial(visit, False)
    )
    total = jnp.sum(tot[...], axis=-1, keepdims=True)
    o_ref[0] = (acc[...] / total).astype(bf16)
    lse_ref[0] = jnp.log(total)


def backward_kernel(
    zs, rows, block, info, q_ref, do_ref, lse_ref, delta_ref, kv_ref, col_ref, row_ref, dq_ref, dkv_ref, acc, dkv
):
    piece, step = pl.program_id(0), pl.program_id(1)
    last = 2 * zs - 1

    @pl.when((piece == 0) & (step == 0))
    def _():
        dkv[...] = jnp.zeros_like(dkv)

    acc[...] = jnp.zeros_like(acc)

    def visit(with_mask, x, ring, half, home, g, first):
        q, do = q_ref[0], do_ref[0]
        k, v = kv_ref[x, ring, half], kv_ref[1 - x, ring, 1 - half]
        bent = jnp.tanh(nt(k, q) * (1.0 / soft_cap))
        weight = jnp.exp(soft_cap * bent - lse_ref[0])
        if with_mask:
            row_at = first + lax.broadcasted_iota(jnp.int32, (rows, block), 1)
            col_at = g * rows + lax.broadcasted_iota(jnp.int32, (rows, block), 0)
            gap = row_at - col_at
            row_doc = jnp.where(home == last, row_ref[0], 0)
            col_doc = jnp.where(g == last, col_ref[...], 0)
            weight = jnp.where((gap >= 0) & (gap < WINDOW) & (row_doc == col_doc), weight, 0.0)
        draw = (weight * (nt(v, do) - delta_ref[0]) * (1.0 - bent * bent)).astype(bf16)
        dkv[x, ring, half] += nn(draw, q)
        dkv[1 - x, ring, 1 - half] += nn(weight.astype(bf16), do)
        acc[...] += tn(draw, k)

    key_loop(
        info, zs, rows, block, functools.partial(visit, True), functools.partial(visit, False)
    )
    dq_ref[0] = acc[...]

    @pl.when((piece == 1) & (step == pl.num_programs(1) - 1))
    def _():
        dkv_ref[...] = dkv[...].astype(bf16)


def whole_block(shape):
    return pl.BlockSpec(shape, lambda i, j, info: (0,) * len(shape))


def attend(info, q, kv, doc_col, doc_row, block):
    unused, zs, unused2, rows, unused3 = kv.shape
    steps = rows // block
    return pl.pallas_call(
        functools.partial(forward_kernel, zs, rows, block),
        grid_spec=pltpu.PrefetchScalarGridSpec(
            num_scalar_prefetch=1,
            grid=(2, steps),
            in_specs=[
                pl.BlockSpec((1, block, HD), lambda i, j, info: (i, j, 0)),
                whole_block(kv.shape),
                pl.BlockSpec((block, 1), lambda i, j, info: (j, 0)),
                whole_block((1, rows)),
            ],
            out_specs=[
                pl.BlockSpec((1, block, HD), lambda i, j, info: (i, j, 0)),
                pl.BlockSpec((1, block, 1), lambda i, j, info: (i, j, 0)),
            ],
            scratch_shapes=[pltpu.VMEM((block, HD), f32), pltpu.VMEM((block, 128), f32)],
        ),
        out_shape=[
            jax.ShapeDtypeStruct((2, rows, HD), bf16),
            jax.ShapeDtypeStruct((2, rows, 1), f32),
        ],
        compiler_params=pltpu.CompilerParams(vmem_limit_bytes=48 * 1024 * 1024),
        cost_estimate=LIGHT,
    )(info, q, kv, doc_col, doc_row)


def attend_back(info, q, d_out, lse, delta, kv, doc_col, doc_row, block):
    unused, zs, unused2, rows, unused3 = kv.shape
    steps = rows // block
    piece_block = pl.BlockSpec((1, block, HD), lambda i, j, info: (i, j, 0))
    row_block = pl.BlockSpec((1, 1, block), lambda i, j, info: (i * steps + j, 0, 0))
    return pl.pallas_call(
        functools.partial(backward_kernel, zs, rows, block),
        grid_spec=pltpu.PrefetchScalarGridSpec(
            num_scalar_prefetch=1,
            grid=(2, steps),
            in_specs=[
                piece_block,
                piece_block,
                row_block,
                row_block,
                whole_block(kv.shape),
                whole_block((rows, 1)),
                pl.BlockSpec((1, 1, block), lambda i, j, info: (j, 0, 0)),
            ],
            out_specs=[piece_block, whole_block(kv.shape)],
            scratch_shapes=[pltpu.VMEM((block, HD), f32), pltpu.VMEM(kv.shape, f32)],
        ),
        out_shape=[
            jax.ShapeDtypeStruct((2, rows, HD), f32),
            jax.ShapeDtypeStruct(kv.shape, bf16),
        ],
        compiler_params=pltpu.CompilerParams(vmem_limit_bytes=56 * 1024 * 1024),
        cost_estimate=LIGHT,
    )(info, q, d_out, lse, delta, kv, doc_col, doc_row)


NN, NT, TN = ((1,), (0,)), ((1,), (1,)), ((0,), (0,))
gelu_slope = math.sqrt(2.0 / math.pi)


def held(shape):
    return pl.BlockSpec(shape, lambda i: (0,) * len(shape), pipeline_mode=pl.Buffered(1))


def row_tiles(tile, columns):
    return pl.BlockSpec((tile, columns), lambda i: (i, 0))


def tiled(body, rows, tile, in_specs, out_columns, out_types, operands):
    return pl.pallas_call(
        body,
        grid=(rows // tile,),
        in_specs=in_specs,
        out_specs=[row_tiles(tile, columns) for columns in out_columns],
        out_shape=[
            jax.ShapeDtypeStruct((rows, columns), kind)
            for columns, kind in zip(out_columns, out_types)
        ],
        compiler_params=pltpu.CompilerParams(vmem_limit_bytes=52 * 1024 * 1024),
        cost_estimate=LIGHT,
    )(*operands)


def product_kernel(dims, count, *refs):
    value = dot(refs[0][...], refs[count][...], dims)
    for i in range(1, count):
        value = value + dot(refs[i][...], refs[count + i][...], dims)
    for added in refs[2 * count : -1]:
        value = value + added[...].astype(f32)
    refs[-1][...] = value.astype(refs[-1].dtype)


def rows_product(lefts, rights, dims, kind, *added):
    lefts, rights = [v if isinstance(v, (list, tuple)) else [v] for v in (lefts, rights)]
    rows = lefts[0].shape[0]
    tile = min(rows, 320)
    columns = rights[0].shape[1 - dims[1][0]]
    specs = [row_tiles(tile, left.shape[1]) for left in lefts]
    specs += [held(right.shape) for right in rights]
    specs += [row_tiles(tile, columns)] * len(added)
    body = functools.partial(product_kernel, dims, len(lefts))
    return tiled(body, rows, tile, specs, [columns], [kind], [*lefts, *rights, *added])[0]


def halves(rows_in):
    return jnp.split(rows_in, 2)


def norm_product_kernel(x_ref, gain_ref, w_ref, h_ref, out_ref):
    field = x_ref[...].astype(f32)
    scale = lax.rsqrt(jnp.mean(field * field, axis=-1, keepdims=True) + epsilon)
    h = (field * scale * gain_ref[...]).astype(bf16)
    h_ref[...] = h
    out_ref[...] = dot(h, w_ref[...], NN)


def norm_product(rows_in, gain, right):
    rows, columns = rows_in.shape
    tile = min(rows, 320)
    specs = [row_tiles(tile, columns), held((1, columns)), held(right.shape)]
    operands = (rows_in, gain[None], right)
    outs, kinds = [columns, right.shape[1]], [bf16, f32]
    return tiled(norm_product_kernel, rows, tile, specs, outs, kinds, operands)


def bend(gate):
    return jnp.tanh(gelu_slope * (gate + 0.044715 * (gate * gate * gate)))


def gated_kernel(h_ref, gate_w, up_w, gate_ref, up_ref, hidden_ref):
    gate = dot(h_ref[...], gate_w[...], NN)
    up = dot(h_ref[...], up_w[...], NN)
    gate_ref[...] = gate
    up_ref[...] = up
    hidden_ref[...] = (0.5 * gate * (1.0 + bend(gate)) * up).astype(bf16)


def gated_product(left, gate_w, up_w):
    rows, depth = left.shape
    tile, columns = min(rows, 160), gate_w.shape[1]
    specs = [row_tiles(tile, depth), held(gate_w.shape), held(up_w.shape)]
    outs, kinds = [columns] * 3, [f32, f32, bf16]
    return tiled(gated_kernel, rows, tile, specs, outs, kinds, (left, gate_w, up_w))


def gated_back_kernel(dm_ref, w_ref, gate_ref, up_ref, d_gate_ref, d_up_ref):
    d_hidden = dot(dm_ref[...], w_ref[...], NN)
    gate, up = gate_ref[...], up_ref[...]
    bent = bend(gate)
    share = 0.5 * (1.0 + bent)
    slope = share + 0.5 * gate * (1.0 - bent * bent) * gelu_slope * (
        1.0 + 3.0 * 0.044715 * (gate * gate)
    )
    d_gate_ref[...] = (d_hidden * up * slope).astype(bf16)
    d_up_ref[...] = (d_hidden * gate * share).astype(bf16)


def gated_back(left, right, gate, up):
    rows, depth = left.shape
    tile, columns = min(rows, 160), gate.shape[1]
    specs = [row_tiles(tile, depth), held(right.shape)] + [row_tiles(tile, columns)] * 2
    outs, kinds = [columns] * 2, [bf16] * 2
    return tiled(gated_back_kernel, rows, tile, specs, outs, kinds, (left, right, gate, up))


def sum_kernel(*refs):
    count = len(refs) // 2
    value = sum(dot(refs[i][...], refs[count + i][...], TN) for i in range(count))
    refs[-1][...] = value.astype(refs[-1].dtype)


def sum_over_rows(pairs, kind=f32):
    lefts, rights = zip(*pairs)
    depth, rows = lefts[0].shape
    tile, columns = 384, rights[0].shape[1]
    left_specs = [pl.BlockSpec((left.shape[0], tile), lambda i: (0, i)) for left in lefts]
    specs = left_specs + [held(right.shape) for right in rights]
    return tiled(sum_kernel, rows, tile, specs, [columns], [kind], lefts + rights)[0]


def shards(
    layer_in,
    segment_ids,
    attn_pre_gain,
    query_weight,
    key_weight,
    value_weight,
    out_weight,
    attn_post_gain,
    ffn_pre_gain,
    gate_weight,
    up_weight,
    down_weight,
    ffn_post_gain,
    out_grad,
):
    unused, rows, width = layer_in.shape
    zs, ts = lax.axis_size("fsdp"), lax.axis_size("tensor")
    x, z, t = lax.axis_index("seq"), lax.axis_index("fsdp"), lax.axis_index("tensor")
    depth = attn_pre_gain.shape[0]
    sub = rows // ts
    units = gate_weight.shape[1] // 2
    first = x == 0

    def in_order(parts):
        return jnp.stack(
            [lax.dynamic_index_in_dim(parts, j ^ t, 1, keepdims=False) for j in range(ts)], axis=1
        )

    def to_exchange(pieces):
        parts = in_order(pieces.reshape(2, ts, sub, -1)).reshape(2, 2, 2, sub, -1)
        return parts.transpose(2, 1, 0, 3, 4).reshape(2 * rows, -1)

    def to_sequence(blocks):
        parts = blocks.reshape(2, 2, 2, sub, -1).transpose(2, 1, 0, 3, 4)
        return in_order(parts.reshape(2, ts, sub, -1)).reshape(2, rows, -1)

    def z_move(value, bits):
        return Move(value, functools.partial(swap, axis="fsdp", bit=bits))

    def gathered(part):
        return lax.all_gather(part, "fsdp", axis=0, tiled=True)

    gate_w, up_w = (
        Move(lax.dynamic_slice_in_dim(weight, x * units, units, 1), gathered)
        for weight in (gate_weight, up_weight)
    )
    down_w = Move(lax.dynamic_slice_in_dim(down_weight, x * units, units, 0).T, gathered)
    down_w.result = gathered(down_w.value)
    w_own = jnp.concatenate(
        [
            lax.dynamic_slice_in_dim(query_weight, x * HD, HD, 1),
            jnp.where(first, key_weight, value_weight),
        ],
        axis=1,
    )
    gains = jnp.concatenate([attn_pre_gain, attn_post_gain, ffn_pre_gain, ffn_post_gain])
    gain_rows = -(-4 * depth // (32 * HD)) * 16
    gains = jnp.pad(gains, (0, gain_rows * 2 * HD - 4 * depth)).reshape(gain_rows, 2 * HD)
    w_own = jnp.concatenate([w_own, gains])
    own_x = in_order(layer_in.reshape(1, ts, sub, width))[0]
    own_x = own_x.reshape(2, 2, sub, width).transpose(1, 0, 2, 3)
    w_own, to_far = lax.optimization_barrier((w_own, own_x[0]))
    ring = [w_own]
    far_move = Move(to_far, swap_x)
    far_move.result = swap_x(to_far)
    for i in range(1, zs):
        final = i == zs - 1
        (block,) = step(
            [ring[-1]], begin=[gate_w] if i == 2 else [], end=[far_move] if final else []
        )
        ring.append(turn(block))
    far_x = far_move.result
    far_x = jnp.concatenate([far_x, swap_core(far_x)]).reshape(rows, width)

    w_out_own = lax.dynamic_slice_in_dim(out_weight, x * HD, HD, 0).T
    out_moves = {j: z_move(w_out_own, j) for j in range(1, zs)}
    def assemble(own, moves):
        whole = jnp.zeros((width, own.shape[1]), bf16)
        whole = lax.dynamic_update_slice_in_dim(whole, own, z * depth, 0)
        for j, parts in moves.items():
            offset = 0
            for part in parts if isinstance(parts, list) else [parts]:
                part = part.result if isinstance(part, Move) else part
                whole = lax.dynamic_update_slice_in_dim(whole, part, (z ^ j) * depth + offset, 0)
                offset += part.shape[0]
        return whole

    w_qkv = jnp.zeros((width, 2 * HD), bf16)
    all_gains = jnp.zeros((zs, 4, depth), bf16)
    for i, part in enumerate(ring):
        place = (z - i) % zs
        w_qkv = lax.dynamic_update_slice_in_dim(w_qkv, part[:depth], place * depth, 0)
        part = part[depth:].reshape(-1)[: 4 * depth].reshape(1, 4, depth)
        all_gains = lax.dynamic_update_slice_in_dim(all_gains, part, place, 0)
    all_gains = all_gains.transpose(1, 0, 2).reshape(4, width).astype(f32)
    pre_gain, post_gain, mlp_pre, mlp_post = (all_gains[i] for i in range(4))
    h_own, own_part = norm_product(own_x.reshape(rows, width), pre_gain, w_qkv)
    h_far, far_part = norm_product(far_x, pre_gain, w_qkv)
    projected = jnp.stack(
        [part.reshape(2, 2, sub, 2 * HD) for part in (own_part, far_part)], axis=2
    )
    projected = to_sequence(projected)
    starts = jnp.stack([x * zs + z, (1 - x) * zs + z]) * rows
    positions = starts[:, None] + jnp.arange(rows, dtype=jnp.int32)[None, :]
    cos_tab, sine_tab = tables(positions.astype(f32))
    kv_cos = jnp.where(first, cos_tab, 1.0)
    kv_sine = jnp.where(first, sine_tab, 0.0)
    q_scale = HD ** (-0.5)
    q_cast = (rotate(projected[..., :HD], cos_tab, sine_tab) * q_scale).astype(bf16)
    kv_ring, kv_far = [rotate(projected[..., HD:], kv_cos, kv_sine).astype(bf16)], []
    for i in range(zs):
        moves = []
        if i == zs - 1:
            moves = [out_moves[j] for j in range(1, zs - 1)] + [up_w]
        (here,) = step([kv_ring[-1]], begin=moves)
        if i < zs - 1:
            kv_ring.append(turn(here))
        kv_far.append(swap_x(here))
    kv_all = jnp.stack(kv_ring + kv_far).reshape(2, zs, 2, rows, HD)

    block = rows // 2 if rows >= 512 else rows
    last_doc = segment_ids.reshape(2 * zs, rows)[-1]
    info = jnp.concatenate([jnp.stack([x, z]), last_doc[::block]]).astype(jnp.int32)
    doc_col, doc_row = last_doc[:, None], last_doc[None, :]
    early_out, late_out = [out_moves[j] for j in range(1, zs - 1)], [out_moves[zs - 1]]
    q_cast, kv_all = step([q_cast, kv_all], begin=late_out, end=early_out + [gate_w])
    mixed, lse = attend(info, q_cast, kv_all, doc_col, doc_row, block)
    (mixed,) = step([mixed], end=late_out)
    w_out = assemble(w_out_own, out_moves)

    o_rows = to_exchange(mixed)
    o_halves = halves(o_rows)
    a_sum = scatter8(
        lambda got: rows_product(o_halves[0], w_out, NT, bf16, got),
        lambda: rows_product(o_halves[1], w_out, NT, bf16),
        {},
    )

    x_own = lax.dynamic_slice_in_dim(layer_in[0], t * sub, sub, 0).astype(f32)
    r_one = x_own + rms_norm(a_sum, post_gain)
    h_two = gather8(rms_norm(r_one, mlp_pre).astype(bf16), {0: ((), [up_w])})
    gate, up, hidden = zip(
        *(gated_product(part, gate_w.result, up_w.result) for part in h_two)
    )
    hidden = step(hidden)
    m_sum = scatter8(
        lambda got: rows_product(hidden[0], down_w.result, NT, bf16, got),
        lambda: rows_product(hidden[1], down_w.result, NT, bf16),
        {},
    )
    layer_own = (r_one + rms_norm(m_sum, mlp_post)).astype(bf16)

    incoming = lax.dynamic_slice_in_dim(out_grad[0], t * sub, sub, 0).astype(f32)
    d_msum, dg_mlp_post = norm_back(m_sum, mlp_post, incoming)
    def scattered(grad):
        return lax.psum_scatter(grad, "fsdp", scatter_dimension=0, tiled=True)

    class Unit:
        def __init__(self, grad, held=False):
            self.sum = Move(grad, scattered)
            if not held:
                self.sum.result = scattered(grad)

        def paired(self):
            self.over = [Move(self.sum.result, swap_x)]
            return self.over

        def parts(self):
            (move,) = self.over
            return move.value, move.result

    class Late:
        def __init__(self, places):
            self.places = places

        def __contains__(self, place):
            return place in self.places

        def __getitem__(self, place):
            return self.places[place]()

    def product(given):
        return sum_over_rows(list(zip(*given)), bf16)

    dm = gather8(d_msum.astype(bf16), {})
    down_work = Move((dm, hidden), product)
    dm = step(dm, begin=[down_work])
    dm = step(dm, end=[down_work])
    down_unit = Unit(down_work.result)
    d_gate, d_up = zip(
        *(gated_back(part, down_w.result, *have) for part, *have in zip(dm, gate, up))
    )
    gate_work, up_work = Move((h_two, d_gate), product), Move((h_two, d_up), product)
    weights = (gate_w.result, up_w.result)
    dh_two = scatter8(
        lambda got: rows_product((d_gate[0], d_up[0]), weights, NT, bf16, got),
        lambda: rows_product((d_gate[1], d_up[1]), weights, NT, bf16),
        {1: ([gate_work], ()), 2: ([up_work], [gate_work])},
    )
    gate_unit = Unit(gate_work.result)
    dr_add, dg_mlp_pre = norm_back(r_one, mlp_pre, dh_two)
    d_resid = incoming + dr_add
    d_asum, dg_post = norm_back(a_sum, post_gain, d_resid)

    (da,) = step([d_asum.astype(bf16)], end=[up_work, down_unit.sum])
    up_unit = Unit(up_work.result, held=True)
    da = gather8(da, {})
    def qkv_grad(rows_in, kind=f32):
        parts = rows_in.reshape(2, 2, 2, sub, HD)
        near = parts[:, :, 0].reshape(rows, HD)
        far = parts[:, :, 1].reshape(rows, HD)
        return sum_over_rows([(h_own, near), (h_far, far)], kind)

    def sends(grad):
        moves = [
            z_move(lax.dynamic_index_in_dim(grad, z ^ j, 0, False).astype(bf16), j)
            for j in range(1, zs)
        ]
        return lax.dynamic_index_in_dim(grad, z, 0, False), moves

    def received(pair_of):
        near, moves = pair_of
        for move in moves:
            near = near + move.result.astype(f32)
        return near.astype(bf16)

    d_mixed = to_sequence(jnp.concatenate([rows_product(part, w_out, NN, bf16) for part in da]))
    out_work = Move((da, o_halves), product)
    da = step(da, begin=[out_work])
    delta = jnp.sum(d_mixed.astype(f32) * mixed.astype(f32), axis=-1)
    steps = rows // block
    layer_y = Move(layer_own, swap_y)
    d_mixed, delta = step([d_mixed, delta], end=[out_work])
    d_mixed, delta = step([d_mixed, delta], begin=down_unit.paired() + [layer_y])
    d_query, dkv_all = attend_back(
        info,
        q_cast,
        d_mixed,
        lse.reshape(2 * steps, 1, block),
        delta.reshape(2 * steps, 1, block),
        kv_all,
        doc_col,
        doc_row.reshape(steps, 1, block),
        block,
    )
    (dkv_all,) = step([dkv_all], end=down_unit.over)
    q_rows = to_exchange(rotate(d_query * q_scale, cos_tab, -sine_tab).astype(bf16))

    q_work = Move(q_rows, lambda part: qkv_grad(part, bf16))
    (dkv_all,) = step([dkv_all], begin=[q_work])
    kept, given = dkv_all[0], dkv_all[1]
    order = list(range(1, zs)) + [0]
    acc = kept[order[0]].astype(f32) + send(given[order[0]], swap_x)
    for n, i in enumerate(order[1:]):
        moved, far = acc.astype(bf16), given[i]
        if n == 0:
            query_work = [
                Move(part, lambda part: rows_product(part, w_qkv[:, :HD], NT, f32))
                for part in halves(q_rows)
            ]
            (far,) = step([far], end=[q_work])
            other_unit = Unit(
                jnp.concatenate([out_work.result, q_work.result], axis=1), held=True
            )
            moved, far = step(
                [moved, far],
                begin=query_work + [other_unit.sum],
                end=[layer_y, gate_unit.sum],
            )
        if n == 1:
            moved, far = step(
                [moved, far], begin=gate_unit.paired() + [up_unit.sum], end=query_work
            )
        if n == len(order) - 2:
            moved, far = step([moved, far], end=gate_unit.over)
        acc = kept[i].astype(f32) + swap_x(far).astype(f32) + turn(moved).astype(f32)
    dkv_cast = rotate(acc, kv_cos, -kv_sine).astype(bf16)
    kv_rows = to_exchange(dkv_cast)
    kv_work = Move(kv_rows, qkv_grad)
    (kv_rows,) = step([kv_rows], begin=[kv_work], end=[other_unit.sum])
    (kv_rows,) = step([kv_rows], begin=other_unit.paired(), end=[kv_work])
    kv_halves = halves(kv_rows)
    kv_back = sends(kv_work.result.reshape(zs, depth, HD))
    layer_pair = jnp.stack([layer_own, layer_y.result])
    layer_core = Move(layer_pair, swap_core)
    w_kv = w_qkv[:, HD:]
    dh_one = scatter8(
        lambda got: rows_product(kv_halves[0], w_kv, NT, bf16, query_work[0].result, got),
        lambda: rows_product(kv_halves[1], w_kv, NT, bf16, query_work[1].result),
        {1: (kv_back[1], other_unit.over)},
    )
    dx_add, dg_pre = norm_back(x_own, pre_gain, dh_one)
    grad_own = (d_resid + dx_add).astype(bf16)
    (grad_own,) = step([grad_own], end=kv_back[1] + [up_unit.sum])
    grad_own, dg_pre = step([grad_own, dg_pre], begin=up_unit.paired())
    grad_pair = jnp.stack([grad_own, swap_y(grad_own)])
    kv_x = Move(received(kv_back), swap_x)
    (grad_pair,) = step([grad_pair], begin=[kv_x, layer_core])
    last_moves = up_unit.over + [kv_x]
    grad_all = jnp.stack([grad_pair, swap_core(grad_pair)], axis=1).reshape(1, ts, sub, width)
    (grad_all,) = step([grad_all], end=last_moves)
    input_grad = in_order(grad_all).reshape(1, rows, width).astype(f32)
    layer_all = jnp.stack([layer_pair, layer_core.result], axis=1).reshape(1, ts, sub, width)
    layer_out = in_order(layer_all).reshape(1, rows, width)

    gain_grads = jnp.stack([dg_pre, dg_post, dg_mlp_pre, dg_mlp_post])
    bits = 1
    while bits < zs:
        gain_grads = gain_grads + swap(gain_grads, "fsdp", bits)
        bits *= 2
    for mover in (swap_y, swap_core, swap_x):
        gain_grads = gain_grads + mover(gain_grads)
    gain_grads = lax.dynamic_slice_in_dim(gain_grads, z * depth, depth, 1)

    def two(even, left, right):
        return jnp.where(
            even, jnp.concatenate([left, right], 1), jnp.concatenate([right, left], 1)
        )

    g_down = two(first, *down_unit.parts()).T.astype(f32)
    g_gate = two(first, *gate_unit.parts()).astype(f32)
    g_up = two(first, *up_unit.parts()).astype(f32)
    near, far = other_unit.parts()
    g_out = two(first, near[:, :HD], far[:, :HD]).T.astype(f32)
    g_query = two(first, near[:, HD:], far[:, HD:]).astype(f32)
    near, far = kv_x.value, kv_x.result
    g_key = jnp.where(first, near, far).astype(f32)
    g_value = jnp.where(first, far, near).astype(f32)
    return (
        layer_out,
        input_grad,
        gain_grads[0],
        g_query,
        g_key,
        g_value,
        g_out,
        gain_grads[1],
        gain_grads[2],
        g_gate,
        g_up,
        g_down,
        gain_grads[3],
    )


def solution(mesh):
    return jax.shard_map(
        shards,
        mesh=mesh,
        in_specs=(
            P(None, ("seq", "fsdp"), None),
            P(),
            P("fsdp"),
            P("fsdp", "tensor"),
            P("fsdp", "tensor"),
            P("fsdp", "tensor"),
            P("tensor", "fsdp"),
            P("fsdp"),
            P("fsdp"),
            P("fsdp", "tensor"),
            P("fsdp", "tensor"),
            P("tensor", "fsdp"),
            P("fsdp"),
            P(None, ("seq", "fsdp"), None),
        ),
        out_specs=(
            P(None, ("seq", "fsdp"), None),
            P(None, ("seq", "fsdp"), None),
            P("fsdp"),
            P("fsdp", "tensor"),
            P("fsdp", "tensor"),
            P("fsdp", "tensor"),
            P("tensor", "fsdp"),
            P("fsdp"),
            P("fsdp"),
            P("fsdp", "tensor"),
            P("fsdp", "tensor"),
            P("tensor", "fsdp"),
            P("fsdp"),
        ),
        check_vma=False,
    )
```

```python
import functools
import math

import jax
import jax.numpy as jnp
from jax import lax
from jax.experimental import pallas as pl
from jax.experimental.layout import Layout, with_layout_constraint
from jax.experimental.pallas import tpu as pltpu
from jax.sharding import PartitionSpec as P

HD = 256
WINDOW = 4096
epsilon = 1e-06
soft_cap = 50.0
f32 = jnp.float32
bf16 = jnp.bfloat16


def swap(value, axis, bit=1):
    return lax.ppermute(value, axis, [(i, i ^ bit) for i in range(lax.axis_size(axis))])


def swap_x(value):
    return swap(value, "seq")


def swap_y(value):
    return swap(value, "tensor", 2)


def swap_core(value):
    return swap(value, "tensor", 1)


def turn(value):
    size = lax.axis_size("fsdp")
    return lax.ppermute(value, "fsdp", [(i, (i + 1) % size) for i in range(size)])


class Move:
    def __init__(self, value, mover):
        self.value, self.mover, self.result = value, mover, None


def step(values, begin=(), end=()):
    values, given, taken = lax.optimization_barrier(
        (list(values), [move.value for move in begin], [move.result for move in end])
    )
    for move, value in zip(begin, given):
        move.value, move.result = value, move.mover(value)
    for move, result in zip(end, taken):
        move.result = result
    return values


def at(plan, place, values):
    return step(values, *plan[place]) if place in plan else step(values)


def gather8(own, plan):
    cut = own.shape[1] // 2
    a, b = at(plan, 0, [own[:, :cut], own[:, cut:]])
    a, b = jnp.stack([a, swap_x(a)]), jnp.stack([b, swap_y(b)])
    a, b = at(plan, 1, [a, b])
    a, b = jnp.stack([a, swap_y(a)]), jnp.stack([b, swap_x(b)], axis=1)
    chip = jnp.concatenate([a, b], axis=-1).reshape(4 * own.shape[0], -1)
    (chip,) = at(plan, 2, [chip])
    return chip, swap_core(chip)


def send(part, mover):
    return mover(part.astype(bf16)).astype(f32)


def scatter8(keep, give, plan):
    (given,) = at(plan, 0, [give()])
    part = keep(swap_core(given))
    rows, width = part.shape[0] // 4, part.shape[1]
    cut = width // 2
    part = part.reshape(2, 2, rows, width)
    a, b = part[..., :cut], part[..., cut:]
    give_a, give_b = at(plan, 1, [a[:, 1], b[1]])
    a = a[:, 0].astype(f32) + swap_x(give_a).astype(f32)
    b = b[0].astype(f32) + swap_y(give_b).astype(f32)
    give_a, give_b = at(plan, 2, [a[1].astype(bf16), b[1].astype(bf16)])
    a = a[0] + swap_y(give_a).astype(f32)
    b = b[0] + swap_x(give_b).astype(f32)
    return jnp.concatenate([a, b], axis=-1)


def rms_norm(field, gain_vec):
    return field * lax.rsqrt(jnp.mean(field * field, axis=-1, keepdims=True) + epsilon) * gain_vec


def norm_back(field, gain_vec, incoming):
    unused, pullback = jax.vjp(rms_norm, field, gain_vec)
    return pullback(incoming)


def tables(positions):
    frequency = jnp.exp(jnp.arange(HD // 2, dtype=f32) * (-2.0 * math.log(10000.0) / HD))
    angles = positions[..., None] * frequency
    return (jnp.cos(angles), jnp.sin(angles))


def rotate(field, cos_tab, sine_tab):
    half_dim = field.shape[-1] // 2
    front, back = field[..., :half_dim], field[..., half_dim:]
    return jnp.concatenate(
        [front * cos_tab - back * sine_tab, back * cos_tab + front * sine_tab], axis=-1
    )


def dot(left, right, dims):
    return lax.dot_general(left, right, (dims, ((), ())), preferred_element_type=f32)


def nn(left, right):
    return dot(left, right, ((1,), (0,)))


def nt(left, right):
    return dot(left, right, ((1,), (1,)))


def tn(left, right):
    return dot(left, right, ((0,), (0,)))


LIGHT = pl.CostEstimate(flops=500_000_000, bytes_accessed=1_000_000, transcendentals=0)


def block_place(info, zs, rows, block):
    x, z = info[0], info[1]
    piece, step = pl.program_id(0), pl.program_id(1)
    home = jnp.where(piece == 0, x, 1 - x) * zs + z
    first = home * rows + step * block
    return x, z, home, first, info[2 + step]


def key_loop(info, zs, rows, block, masked, plain):
    x, z, home, first, first_doc = block_place(info, zs, rows, block)
    last = 2 * zs - 1
    low = jnp.maximum(first - (WINDOW - 1), 0) // rows
    low = jnp.where((home == last) & (first_doc > 0), last, low)

    def visit(g, carry):
        half = (g >= zs).astype(jnp.int32)
        ring = lax.rem(z - (g - half * zs) + zs, zs)
        far = first + block - 1 - g * rows >= WINDOW
        need = (g == home) | far | (home == last)

        @pl.when(need)
        def _():
            masked(x, ring, half, home, g, first)

        @pl.when(jnp.logical_not(need))
        def _():
            plain(x, ring, half, home, g, first)

        return carry

    lax.fori_loop(low, home + 1, visit, 0)


def forward_kernel(zs, rows, block, info, q_ref, kv_ref, col_ref, row_ref, o_ref, lse_ref, acc, tot):
    acc[...] = jnp.zeros_like(acc)
    tot[...] = jnp.zeros_like(tot)
    last = 2 * zs - 1

    def visit(with_mask, x, ring, half, home, g, first):
        raw = nt(q_ref[0], kv_ref[x, ring, half])
        weight = jnp.exp(soft_cap * jnp.tanh(raw * (1.0 / soft_cap)))
        if with_mask:
            row_at = first + lax.broadcasted_iota(jnp.int32, (block, rows), 0)
            col_at = g * rows + lax.broadcasted_iota(jnp.int32, (block, rows), 1)
            gap = row_at - col_at
            row_doc = jnp.where(home == last, col_ref[...], 0)
            col_doc = jnp.where(g == last, row_ref[...], 0)
            weight = jnp.where((gap >= 0) & (gap < WINDOW) & (row_doc == col_doc), weight, 0.0)
        part = weight[:, :128]
        for lane in range(128, rows, 128):
            width = min(128, rows - lane)
            if width < 128:
                tail = jnp.concatenate(
                    [weight[:, lane:], jnp.zeros((block, 128 - width), f32)], axis=1
                )
            else:
                tail = weight[:, lane : lane + 128]
            part = part + tail
        tot[...] += part
        acc[...] += nn(weight.astype(bf16), kv_ref[1 - x, ring, 1 - half])

    key_loop(
        info, zs, rows, block, functools.partial(visit, True), functools.partial(visit, False)
    )
    total = jnp.sum(tot[...], axis=-1, keepdims=True)
    o_ref[0] = (acc[...] / total).astype(bf16)
    lse_ref[0] = jnp.log(total)


def backward_kernel(
    zs, rows, block, info, q_ref, do_ref, lse_ref, delta_ref, kv_ref, col_ref, row_ref, dq_ref, dkv_ref, acc, dkv
):
    piece, step = pl.program_id(0), pl.program_id(1)
    last = 2 * zs - 1

    @pl.when((piece == 0) & (step == 0))
    def _():
        dkv[...] = jnp.zeros_like(dkv)

    acc[...] = jnp.zeros_like(acc)

    def visit(with_mask, x, ring, half, home, g, first):
        q, do = q_ref[0], do_ref[0]
        k, v = kv_ref[x, ring, half], kv_ref[1 - x, ring, 1 - half]
        bent = jnp.tanh(nt(k, q) * (1.0 / soft_cap))
        weight = jnp.exp(soft_cap * bent - lse_ref[0])
        if with_mask:
            row_at = first + lax.broadcasted_iota(jnp.int32, (rows, block), 1)
            col_at = g * rows + lax.broadcasted_iota(jnp.int32, (rows, block), 0)
            gap = row_at - col_at
            row_doc = jnp.where(home == last, row_ref[0], 0)
            col_doc = jnp.where(g == last, col_ref[...], 0)
            weight = jnp.where((gap >= 0) & (gap < WINDOW) & (row_doc == col_doc), weight, 0.0)
        draw = (weight * (nt(v, do) - delta_ref[0]) * (1.0 - bent * bent)).astype(bf16)
        dkv[x, ring, half] += nn(draw, q)
        dkv[1 - x, ring, 1 - half] += nn(weight.astype(bf16), do)
        acc[...] += tn(draw, k)

    key_loop(
        info, zs, rows, block, functools.partial(visit, True), functools.partial(visit, False)
    )
    dq_ref[0] = acc[...]

    @pl.when((piece == 1) & (step == pl.num_programs(1) - 1))
    def _():
        dkv_ref[...] = dkv[...].astype(bf16)


def whole_block(shape):
    return pl.BlockSpec(shape, lambda i, j, info: (0,) * len(shape))


def attend(info, q, kv, doc_col, doc_row, block):
    unused, zs, unused2, rows, unused3 = kv.shape
    steps = rows // block
    return pl.pallas_call(
        functools.partial(forward_kernel, zs, rows, block),
        grid_spec=pltpu.PrefetchScalarGridSpec(
            num_scalar_prefetch=1,
            grid=(2, steps),
            in_specs=[
                pl.BlockSpec((1, block, HD), lambda i, j, info: (i, j, 0)),
                whole_block(kv.shape),
                pl.BlockSpec((block, 1), lambda i, j, info: (j, 0)),
                whole_block((1, rows)),
            ],
            out_specs=[
                pl.BlockSpec((1, block, HD), lambda i, j, info: (i, j, 0)),
                pl.BlockSpec((1, block, 1), lambda i, j, info: (i, j, 0)),
            ],
            scratch_shapes=[pltpu.VMEM((block, HD), f32), pltpu.VMEM((block, 128), f32)],
        ),
        out_shape=[
            jax.ShapeDtypeStruct((2, rows, HD), bf16),
            jax.ShapeDtypeStruct((2, rows, 1), f32),
        ],
        compiler_params=pltpu.CompilerParams(vmem_limit_bytes=48 * 1024 * 1024),
        cost_estimate=LIGHT,
    )(info, q, kv, doc_col, doc_row)


def attend_back(info, q, d_out, lse, delta, kv, doc_col, doc_row, block):
    unused, zs, unused2, rows, unused3 = kv.shape
    steps = rows // block
    piece_block = pl.BlockSpec((1, block, HD), lambda i, j, info: (i, j, 0))
    row_block = pl.BlockSpec((1, 1, block), lambda i, j, info: (i * steps + j, 0, 0))
    return pl.pallas_call(
        functools.partial(backward_kernel, zs, rows, block),
        grid_spec=pltpu.PrefetchScalarGridSpec(
            num_scalar_prefetch=1,
            grid=(2, steps),
            in_specs=[
                piece_block,
                piece_block,
                row_block,
                row_block,
                whole_block(kv.shape),
                whole_block((rows, 1)),
                pl.BlockSpec((1, 1, block), lambda i, j, info: (j, 0, 0)),
            ],
            out_specs=[piece_block, whole_block(kv.shape)],
            scratch_shapes=[pltpu.VMEM((block, HD), f32), pltpu.VMEM(kv.shape, f32)],
        ),
        out_shape=[
            jax.ShapeDtypeStruct((2, rows, HD), f32),
            jax.ShapeDtypeStruct(kv.shape, bf16),
        ],
        compiler_params=pltpu.CompilerParams(vmem_limit_bytes=56 * 1024 * 1024),
        cost_estimate=LIGHT,
    )(info, q, d_out, lse, delta, kv, doc_col, doc_row)


NN, NT, TN = ((1,), (0,)), ((1,), (1,)), ((0,), (0,))
gelu_slope = math.sqrt(2.0 / math.pi)


def held(shape):
    return pl.BlockSpec(shape, lambda i: (0,) * len(shape), pipeline_mode=pl.Buffered(1))


def row_tiles(tile, columns):
    return pl.BlockSpec((tile, columns), lambda i: (i, 0))


def tiled(body, rows, tile, in_specs, out_columns, out_types, operands):
    return pl.pallas_call(
        body,
        grid=(rows // tile,),
        in_specs=in_specs,
        out_specs=[row_tiles(tile, columns) for columns in out_columns],
        out_shape=[
            jax.ShapeDtypeStruct((rows, columns), kind)
            for columns, kind in zip(out_columns, out_types)
        ],
        compiler_params=pltpu.CompilerParams(vmem_limit_bytes=52 * 1024 * 1024),
        cost_estimate=LIGHT,
    )(*operands)


def product_kernel(dims, count, *refs):
    value = dot(refs[0][...], refs[count][...], dims)
    for i in range(1, count):
        value = value + dot(refs[i][...], refs[count + i][...], dims)
    for added in refs[2 * count : -1]:
        value = value + added[...].astype(f32)
    refs[-1][...] = value.astype(refs[-1].dtype)


def rows_product(lefts, rights, dims, kind, *added):
    lefts, rights = [v if isinstance(v, (list, tuple)) else [v] for v in (lefts, rights)]
    rows = lefts[0].shape[0]
    tile = min(rows, 320)
    columns = rights[0].shape[1 - dims[1][0]]
    specs = [row_tiles(tile, left.shape[1]) for left in lefts]
    specs += [held(right.shape) for right in rights]
    specs += [row_tiles(tile, columns)] * len(added)
    body = functools.partial(product_kernel, dims, len(lefts))
    return tiled(body, rows, tile, specs, [columns], [kind], [*lefts, *rights, *added])[0]


def halves(rows_in):
    return jnp.split(rows_in, 2)


def norm_product_kernel(x_ref, gain_ref, w_ref, h_ref, out_ref):
    field = x_ref[...].astype(f32)
    scale = lax.rsqrt(jnp.mean(field * field, axis=-1, keepdims=True) + epsilon)
    h = (field * scale * gain_ref[...]).astype(bf16)
    h_ref[...] = h
    out_ref[...] = dot(h, w_ref[...], NN)


def norm_product(rows_in, gain, right):
    rows, columns = rows_in.shape
    tile = min(rows, 320)
    specs = [row_tiles(tile, columns), held((1, columns)), held(right.shape)]
    operands = (rows_in, gain[None], right)
    outs, kinds = [columns, right.shape[1]], [bf16, f32]
    return tiled(norm_product_kernel, rows, tile, specs, outs, kinds, operands)


def bend(gate):
    return jnp.tanh(gelu_slope * (gate + 0.044715 * (gate * gate * gate)))


def gated_kernel(h_ref, gate_w, up_w, gate_ref, up_ref, hidden_ref):
    gate = dot(h_ref[...], gate_w[...], NN)
    up = dot(h_ref[...], up_w[...], NN)
    gate_ref[...] = gate
    up_ref[...] = up
    hidden_ref[...] = (0.5 * gate * (1.0 + bend(gate)) * up).astype(bf16)


def gated_product(left, gate_w, up_w):
    rows, depth = left.shape
    tile, columns = min(rows, 160), gate_w.shape[1]
    specs = [row_tiles(tile, depth), held(gate_w.shape), held(up_w.shape)]
    outs, kinds = [columns] * 3, [f32, f32, bf16]
    return tiled(gated_kernel, rows, tile, specs, outs, kinds, (left, gate_w, up_w))


def gated_back_kernel(dm_ref, w_ref, gate_ref, up_ref, d_gate_ref, d_up_ref):
    d_hidden = dot(dm_ref[...], w_ref[...], NN)
    gate, up = gate_ref[...], up_ref[...]
    bent = bend(gate)
    share = 0.5 * (1.0 + bent)
    slope = share + 0.5 * gate * (1.0 - bent * bent) * gelu_slope * (
        1.0 + 3.0 * 0.044715 * (gate * gate)
    )
    d_gate_ref[...] = (d_hidden * up * slope).astype(bf16)
    d_up_ref[...] = (d_hidden * gate * share).astype(bf16)


def gated_back(left, right, gate, up):
    rows, depth = left.shape
    tile, columns = min(rows, 160), gate.shape[1]
    specs = [row_tiles(tile, depth), held(right.shape)] + [row_tiles(tile, columns)] * 2
    outs, kinds = [columns] * 2, [bf16] * 2
    return tiled(gated_back_kernel, rows, tile, specs, outs, kinds, (left, right, gate, up))


def sum_kernel(*refs):
    count = len(refs) // 2
    value = sum(dot(refs[i][...], refs[count + i][...], TN) for i in range(count))
    refs[-1][...] = value.astype(refs[-1].dtype)


def sum_over_rows(pairs, kind=f32):
    lefts, rights = zip(*pairs)
    depth, rows = lefts[0].shape
    tile, columns = 384, rights[0].shape[1]
    left_specs = [pl.BlockSpec((left.shape[0], tile), lambda i: (0, i)) for left in lefts]
    specs = left_specs + [held(right.shape) for right in rights]
    return tiled(sum_kernel, rows, tile, specs, [columns], [kind], lefts + rights)[0]


def shards(
    layer_in,
    segment_ids,
    attn_pre_gain,
    query_weight,
    key_weight,
    value_weight,
    out_weight,
    attn_post_gain,
    ffn_pre_gain,
    gate_weight,
    up_weight,
    down_weight,
    ffn_post_gain,
    out_grad,
):
    unused, rows, width = layer_in.shape
    zs, ts = lax.axis_size("fsdp"), lax.axis_size("tensor")
    x, z, t = lax.axis_index("seq"), lax.axis_index("fsdp"), lax.axis_index("tensor")
    depth = attn_pre_gain.shape[0]
    sub = rows // ts
    units = gate_weight.shape[1] // 2
    first = x == 0

    def in_order(parts):
        return jnp.stack(
            [lax.dynamic_index_in_dim(parts, j ^ t, 1, keepdims=False) for j in range(ts)], axis=1
        )

    def to_exchange(pieces):
        parts = in_order(pieces.reshape(2, ts, sub, -1)).reshape(2, 2, 2, sub, -1)
        return parts.transpose(2, 1, 0, 3, 4).reshape(2 * rows, -1)

    def to_sequence(blocks):
        parts = blocks.reshape(2, 2, 2, sub, -1).transpose(2, 1, 0, 3, 4)
        return in_order(parts.reshape(2, ts, sub, -1)).reshape(2, rows, -1)

    def z_move(value, bits):
        return Move(value, functools.partial(swap, axis="fsdp", bit=bits))

    def gathered(part):
        return lax.all_gather(part, "fsdp", axis=0, tiled=True)

    gate_w, up_w = (
        Move(lax.dynamic_slice_in_dim(weight, x * units, units, 1), gathered)
        for weight in (gate_weight, up_weight)
    )
    down_w = Move(lax.dynamic_slice_in_dim(down_weight, x * units, units, 0).T, gathered)
    down_w.result = gathered(down_w.value)
    w_own = jnp.concatenate(
        [
            lax.dynamic_slice_in_dim(query_weight, x * HD, HD, 1),
            jnp.where(first, key_weight, value_weight),
        ],
        axis=1,
    )
    gains = jnp.concatenate([attn_pre_gain, attn_post_gain, ffn_pre_gain, ffn_post_gain])
    gain_rows = -(-4 * depth // (32 * HD)) * 16
    gains = jnp.pad(gains, (0, gain_rows * 2 * HD - 4 * depth)).reshape(gain_rows, 2 * HD)
    w_own = jnp.concatenate([w_own, gains])
    w_own, layer_in = lax.optimization_barrier((w_own, layer_in))
    own_x = in_order(layer_in.reshape(1, ts, sub, width))[0]
    own_x = own_x.reshape(2, 2, sub, width).transpose(1, 0, 2, 3)
    to_far = own_x[0]
    ring = [w_own]
    far_move = Move(to_far, swap_x)
    far_move.result = swap_x(to_far)
    for i in range(1, zs):
        final = i == zs - 1
        (block,) = step(
            [ring[-1]], begin=[gate_w] if i == 2 else [], end=[far_move] if final else []
        )
        ring.append(turn(block))
    far_x = far_move.result
    far_x = jnp.concatenate([far_x, swap_core(far_x)]).reshape(rows, width)

    w_out_own = lax.dynamic_slice_in_dim(out_weight, x * HD, HD, 0).T
    out_moves = {j: z_move(w_out_own, j) for j in range(1, zs)}
    def assemble(own, moves):
        whole = jnp.zeros((width, own.shape[1]), bf16)
        whole = lax.dynamic_update_slice_in_dim(whole, own, z * depth, 0)
        for j, parts in moves.items():
            offset = 0
            for part in parts if isinstance(parts, list) else [parts]:
                part = part.result if isinstance(part, Move) else part
                whole = lax.dynamic_update_slice_in_dim(whole, part, (z ^ j) * depth + offset, 0)
                offset += part.shape[0]
        return whole

    w_qkv = jnp.zeros((width, 2 * HD), bf16)
    all_gains = jnp.zeros((zs, 4, depth), bf16)
    for i, part in enumerate(ring):
        place = (z - i) % zs
        w_qkv = lax.dynamic_update_slice_in_dim(w_qkv, part[:depth], place * depth, 0)
        part = part[depth:].reshape(-1)[: 4 * depth].reshape(1, 4, depth)
        all_gains = lax.dynamic_update_slice_in_dim(all_gains, part, place, 0)
    all_gains = all_gains.transpose(1, 0, 2).reshape(4, width).astype(f32)
    pre_gain, post_gain, mlp_pre, mlp_post = (all_gains[i] for i in range(4))
    h_own, own_part = norm_product(own_x.reshape(rows, width), pre_gain, w_qkv)
    h_far, far_part = norm_product(far_x, pre_gain, w_qkv)
    projected = jnp.stack(
        [part.reshape(2, 2, sub, 2 * HD) for part in (own_part, far_part)], axis=2
    )
    projected = to_sequence(projected)
    starts = jnp.stack([x * zs + z, (1 - x) * zs + z]) * rows
    positions = starts[:, None] + jnp.arange(rows, dtype=jnp.int32)[None, :]
    cos_tab, sine_tab = tables(positions.astype(f32))
    kv_cos = jnp.where(first, cos_tab, 1.0)
    kv_sine = jnp.where(first, sine_tab, 0.0)
    q_scale = HD ** (-0.5)
    q_cast = (rotate(projected[..., :HD], cos_tab, sine_tab) * q_scale).astype(bf16)
    kv_ring, kv_far = [rotate(projected[..., HD:], kv_cos, kv_sine).astype(bf16)], []
    for i in range(zs):
        moves = []
        if i == zs - 1:
            moves = [out_moves[j] for j in range(1, zs - 1)] + [up_w]
        (here,) = step([kv_ring[-1]], begin=moves)
        if i < zs - 1:
            kv_ring.append(turn(here))
        kv_far.append(swap_x(here))
    kv_all = jnp.stack(kv_ring + kv_far).reshape(2, zs, 2, rows, HD)

    block = rows // 2 if rows >= 512 else rows
    last_doc = segment_ids.reshape(2 * zs, rows)[-1]
    info = jnp.concatenate([jnp.stack([x, z]), last_doc[::block]]).astype(jnp.int32)
    doc_col, doc_row = last_doc[:, None], last_doc[None, :]
    early_out, late_out = [out_moves[j] for j in range(1, zs - 1)], [out_moves[zs - 1]]
    q_cast, kv_all = step([q_cast, kv_all], begin=late_out, end=early_out + [gate_w])
    mixed, lse = attend(info, q_cast, kv_all, doc_col, doc_row, block)
    (mixed,) = step([mixed], end=late_out)
    w_out = assemble(w_out_own, out_moves)

    o_rows = to_exchange(mixed)
    o_halves = halves(o_rows)
    a_sum = scatter8(
        lambda got: rows_product(o_halves[0], w_out, NT, bf16, got),
        lambda: rows_product(o_halves[1], w_out, NT, bf16),
        {},
    )

    x_own = lax.dynamic_slice_in_dim(layer_in[0], t * sub, sub, 0).astype(f32)
    r_one = x_own + rms_norm(a_sum, post_gain)
    h_two = gather8(rms_norm(r_one, mlp_pre).astype(bf16), {0: ((), [up_w])})
    gate, up, hidden = zip(
        *(gated_product(part, gate_w.result, up_w.result) for part in h_two)
    )
    hidden = step(hidden)
    m_sum = scatter8(
        lambda got: rows_product(hidden[0], down_w.result, NT, bf16, got),
        lambda: rows_product(hidden[1], down_w.result, NT, bf16),
        {},
    )
    layer_own = (r_one + rms_norm(m_sum, mlp_post)).astype(bf16)

    incoming = lax.dynamic_slice_in_dim(out_grad[0], t * sub, sub, 0).astype(f32)
    d_msum, dg_mlp_post = norm_back(m_sum, mlp_post, incoming)
    def scattered(grad):
        return lax.psum_scatter(grad, "fsdp", scatter_dimension=0, tiled=True)

    class Unit:
        def __init__(self, grad, held=False):
            self.sum = Move(grad, scattered)
            if not held:
                self.sum.result = scattered(grad)

        def paired(self):
            self.over = [Move(self.sum.result, swap_x)]
            return self.over

        def parts(self):
            (move,) = self.over
            return move.value, move.result

    class Late:
        def __init__(self, places):
            self.places = places

        def __contains__(self, place):
            return place in self.places

        def __getitem__(self, place):
            return self.places[place]()

    def product(given):
        return sum_over_rows(list(zip(*given)), bf16)

    dm = gather8(d_msum.astype(bf16), {})
    down_work = Move((dm, hidden), product)
    dm = step(dm, begin=[down_work])
    dm = step(dm, end=[down_work])
    down_unit = Unit(down_work.result)
    d_gate, d_up = zip(
        *(gated_back(part, down_w.result, *have) for part, *have in zip(dm, gate, up))
    )
    gate_work, up_work = Move((h_two, d_gate), product), Move((h_two, d_up), product)
    weights = (gate_w.result, up_w.result)
    dh_two = scatter8(
        lambda got: rows_product((d_gate[0], d_up[0]), weights, NT, bf16, got),
        lambda: rows_product((d_gate[1], d_up[1]), weights, NT, bf16),
        {1: ([gate_work], ()), 2: ([up_work], [gate_work])},
    )
    gate_unit = Unit(gate_work.result)
    dr_add, dg_mlp_pre = norm_back(r_one, mlp_pre, dh_two)
    d_resid = incoming + dr_add
    d_asum, dg_post = norm_back(a_sum, post_gain, d_resid)

    (da,) = step([d_asum.astype(bf16)], end=[up_work, down_unit.sum])
    up_unit = Unit(up_work.result, held=True)
    da = gather8(da, {})
    def qkv_grad(rows_in, kind=f32):
        parts = rows_in.reshape(2, 2, 2, sub, HD)
        near = parts[:, :, 0].reshape(rows, HD)
        far = parts[:, :, 1].reshape(rows, HD)
        return sum_over_rows([(h_own, near), (h_far, far)], kind)

    def sends(grad):
        moves = [
            z_move(lax.dynamic_index_in_dim(grad, z ^ j, 0, False).astype(bf16), j)
            for j in range(1, zs)
        ]
        return lax.dynamic_index_in_dim(grad, z, 0, False), moves

    def received(pair_of):
        near, moves = pair_of
        for move in moves:
            near = near + move.result.astype(f32)
        return near.astype(bf16)

    d_mixed = to_sequence(jnp.concatenate([rows_product(part, w_out, NN, bf16) for part in da]))
    out_work = Move((da, o_halves), product)
    da = step(da, begin=[out_work])
    delta = jnp.sum(d_mixed.astype(f32) * mixed.astype(f32), axis=-1)
    steps = rows // block
    layer_y = Move(layer_own, swap_y)
    d_mixed, delta = step([d_mixed, delta], end=[out_work])
    d_mixed, delta = step([d_mixed, delta], begin=down_unit.paired() + [layer_y])
    d_query, dkv_all = attend_back(
        info,
        q_cast,
        d_mixed,
        lse.reshape(2 * steps, 1, block),
        delta.reshape(2 * steps, 1, block),
        kv_all,
        doc_col,
        doc_row.reshape(steps, 1, block),
        block,
    )
    (dkv_all,) = step([dkv_all], end=down_unit.over)
    q_rows = to_exchange(rotate(d_query * q_scale, cos_tab, -sine_tab).astype(bf16))

    q_work = Move(q_rows, lambda part: qkv_grad(part, bf16))
    (dkv_all,) = step([dkv_all], begin=[q_work])
    kept, given = dkv_all[0], dkv_all[1]
    order = list(range(1, zs)) + [0]
    acc = kept[order[0]].astype(f32) + send(given[order[0]], swap_x)
    for n, i in enumerate(order[1:]):
        moved, far = acc.astype(bf16), given[i]
        if n == 0:
            query_work = [
                Move(part, lambda part: rows_product(part, w_qkv[:, :HD], NT, f32))
                for part in halves(q_rows)
            ]
            (far,) = step([far], end=[q_work])
            other_unit = Unit(
                jnp.concatenate([out_work.result, q_work.result], axis=1), held=True
            )
            moved, far = step(
                [moved, far],
                begin=query_work + [other_unit.sum],
                end=[layer_y, gate_unit.sum],
            )
        if n == 1:
            moved, far = step(
                [moved, far], begin=gate_unit.paired() + [up_unit.sum], end=query_work
            )
        if n == len(order) - 2:
            moved, far = step([moved, far], end=gate_unit.over)
        acc = kept[i].astype(f32) + swap_x(far).astype(f32) + turn(moved).astype(f32)
    dkv_cast = rotate(acc, kv_cos, -kv_sine).astype(bf16)
    kv_rows = to_exchange(dkv_cast)
    kv_work = Move(kv_rows, qkv_grad)
    (kv_rows,) = step([kv_rows], begin=[kv_work], end=[other_unit.sum])
    (kv_rows,) = step([kv_rows], begin=other_unit.paired(), end=[kv_work])
    kv_halves = halves(kv_rows)
    kv_back = sends(kv_work.result.reshape(zs, depth, HD))
    layer_pair = jnp.stack([layer_own, layer_y.result])
    layer_core = Move(layer_pair, swap_core)
    w_kv = w_qkv[:, HD:]
    dh_one = scatter8(
        lambda got: rows_product(kv_halves[0], w_kv, NT, bf16, query_work[0].result, got),
        lambda: rows_product(kv_halves[1], w_kv, NT, bf16, query_work[1].result),
        {1: (kv_back[1], other_unit.over)},
    )
    dx_add, dg_pre = norm_back(x_own, pre_gain, dh_one)
    grad_own = (d_resid + dx_add).astype(bf16)
    (grad_own,) = step([grad_own], end=kv_back[1] + [up_unit.sum])
    grad_own, dg_pre = step([grad_own, dg_pre], begin=up_unit.paired())
    grad_pair = jnp.stack([grad_own, swap_y(grad_own)])
    kv_x = Move(received(kv_back), swap_x)
    (grad_pair,) = step([grad_pair], begin=[kv_x, layer_core])
    last_moves = up_unit.over + [kv_x]
    grad_all = jnp.stack([grad_pair, swap_core(grad_pair)], axis=1).reshape(1, ts, sub, width)
    (grad_all,) = step([grad_all], end=last_moves)
    input_grad = in_order(grad_all).reshape(1, rows, width).astype(f32)
    layer_all = jnp.stack([layer_pair, layer_core.result], axis=1).reshape(1, ts, sub, width)
    layer_out = in_order(layer_all).reshape(1, rows, width)

    gain_grads = jnp.stack([dg_pre, dg_post, dg_mlp_pre, dg_mlp_post])
    bits = 1
    while bits < zs:
        gain_grads = gain_grads + swap(gain_grads, "fsdp", bits)
        bits *= 2
    for mover in (swap_y, swap_core, swap_x):
        gain_grads = gain_grads + mover(gain_grads)
    gain_grads = lax.dynamic_slice_in_dim(gain_grads, z * depth, depth, 1)

    def two(even, left, right):
        return jnp.where(
            even, jnp.concatenate([left, right], 1), jnp.concatenate([right, left], 1)
        )

    g_down = two(first, *down_unit.parts()).T.astype(f32)
    g_gate = two(first, *gate_unit.parts()).astype(f32)
    g_up = two(first, *up_unit.parts()).astype(f32)
    near, far = other_unit.parts()
    g_out = two(first, near[:, :HD], far[:, :HD]).T.astype(f32)
    g_query = two(first, near[:, HD:], far[:, HD:]).astype(f32)
    near, far = kv_x.value, kv_x.result
    g_key = jnp.where(first, near, far).astype(f32)
    g_value = jnp.where(first, far, near).astype(f32)
    return (
        layer_out,
        input_grad,
        gain_grads[0],
        g_query,
        g_key,
        g_value,
        g_out,
        gain_grads[1],
        gain_grads[2],
        g_gate,
        g_up,
        g_down,
        gain_grads[3],
    )


def solution(mesh):
    return jax.shard_map(
        shards,
        mesh=mesh,
        in_specs=(
            P(None, ("seq", "fsdp"), None),
            P(),
            P("fsdp"),
            P("fsdp", "tensor"),
            P("fsdp", "tensor"),
            P("fsdp", "tensor"),
            P("tensor", "fsdp"),
            P("fsdp"),
            P("fsdp"),
            P("fsdp", "tensor"),
            P("fsdp", "tensor"),
            P("tensor", "fsdp"),
            P("fsdp"),
            P(None, ("seq", "fsdp"), None),
        ),
        out_specs=(
            P(None, ("seq", "fsdp"), None),
            P(None, ("seq", "fsdp"), None),
            P("fsdp"),
            P("fsdp", "tensor"),
            P("fsdp", "tensor"),
            P("fsdp", "tensor"),
            P("tensor", "fsdp"),
            P("fsdp"),
            P("fsdp"),
            P("fsdp", "tensor"),
            P("fsdp", "tensor"),
            P("tensor", "fsdp"),
            P("fsdp"),
        ),
        check_vma=False,
    )
```
